32 devices in a mesh: seq: 4 (over y, x), mp: 8 (over z, core).
Axes of the slice: x: 2, y: 2, z: 4, core: 2. Of those that a mesh axis runs over, the one named last changes fastest.
Arguments:
- tokens: bfloat16 [512, 4096], P('seq', 'mp'), may hold values from -68 to 68
- w_qkv: bfloat16 [3, 4096, 4096], P(None, None, 'mp'), may hold values from -0.09375 to 0.09375
- w_pos: bfloat16 [4096, 4096], P(None, 'mp'), may hold values from -0.09375 to 0.09375
- w_out: bfloat16 [4096, 4096], P('mp'), may hold values from -0.09375 to 0.09375
- content_bias: float32 [32, 128], P('mp'), may hold values from -4 to 4
- position_bias: float32 [32, 128], P('mp'), may hold values from -4 to 4
- doc_ids: int32 [512], P('seq'), may hold values from 0 to 3, never falling along the last dimension, each value on 1 to 256 neighbouring positions
Outputs:
- attn_out: bfloat16 [512, 4096], P('seq', 'mp')
The draws below stay inside these ranges and needn't reach their ends.
All inputs are finite; a program needn't handle non-finite values.
Results may differ from the reference program's by a relative error of at most 0.0067.
Values may be sent and summed in bfloat16 or wider, within the bound.
No kernel may reach another device: no remote copies, remote signals or barrier semaphores. Data moves between devices by JAX's collectives and lax.ppermute only.
A program may use at most 64 MiB of HBM per device.

```python
import math
import jax
import jax.numpy as jnp
import numpy as np
from jax import lax

D = 4096
HEADS = 32
HEAD_DIM = 128
SEG = 128
TOKENS = 512


def draw_tokens(key, part):
    first = jax.random.fold_in(key, 0)
    values = jnp.clip(jax.random.normal(first, (TOKENS, D), jnp.float32), -6.0, 6.0)
    return values.astype(jnp.bfloat16)


def block_levels(rng, shape, cuts, smallest, largest):
    gain = 1.0
    for dim, parts in cuts:
        steps = jax.random.uniform(jax.random.fold_in(jax.random.fold_in(rng, 6), dim), (parts,), jnp.float32, smallest / len(cuts), largest / len(cuts))
        gain = gain * jnp.repeat(jnp.exp(steps), shape[dim] // parts).reshape((-1,) + (1,) * (len(shape) - 1 - dim))
    return gain


def length_profile(count, total, most, skew):
    weights = [(1 << 20) // math.isqrt(rank ** skew) + 1 for rank in range(2, count + 1)]
    spare, given = total - most - (count - 1), [1] * (count - 1)
    while spare > 0:
        movable = [i for i in range(count - 1) if given[i] < most]
        mass, remaining = sum([weights[i] for i in movable]), spare
        for i in movable:
            addition = min(most - given[i], max(1, remaining * weights[i] // mass), spare)
            given[i] = given[i] + addition
            spare = spare - addition
    return np.array([most] + given)


def uneven_parts(stream_key, amount, total, bound, skew):
    if amount == 2:
        one = jax.random.randint(stream_key, (), max(1, total - bound), min(bound, total - 1) + 1)
        return jnp.stack([one, total - one])
    lengths = jnp.asarray(length_profile(amount, total, bound, skew), jnp.int32)
    twos = (amount - 1) // 2
    source_of, taker = lengths[1:1 + 2 * twos:2], lengths[2:2 + 2 * twos:2]
    slack = jnp.minimum(source_of - 1, bound - taker)
    moved = jax.random.randint(jax.random.fold_in(stream_key, 1), (twos,), 0, 1 << 20) % (slack + 1)
    lengths = lengths.at[1:1 + 2 * twos:2].set(source_of - moved).at[2:2 + 2 * twos:2].set(taker + moved)
    return lengths[jax.random.permutation(jax.random.fold_in(stream_key, 2), amount)]


def normal_values(rng, extent, scale, most, cuts=(), kind=jnp.bfloat16):
    values = jax.random.normal(rng, extent, jnp.float32) * scale
    if len(cuts) > 0:
        values = block_levels(rng, extent, cuts, -0.22, 0.18) * values
    return jnp.clip(values, min=-most, max=most).astype(kind)


def setup_inputs(seed: int = 0) -> dict:
    key_list = jax.random.split(jax.random.key(seed), 8)
    tokens = draw_tokens(jax.random.fold_in(key_list[7], 71), 0)
    w_qkv = normal_values(key_list[1], (3, D, D), D ** -0.5, 0.09375, ((2, 8),))
    w_pos = normal_values(key_list[2], (D, D), D ** -0.5, 0.09375, ((1, 8),))
    w_out = normal_values(key_list[3], (D, D), D ** -0.5, 0.09375, ((0, 8),))
    content_bias = normal_values(key_list[4], (HEADS, HEAD_DIM), 1.0, 4.0, ((0, 8),), jnp.float32)
    position_bias = normal_values(key_list[5], (HEADS, HEAD_DIM), 1.0, 4.0, ((0, 8),), jnp.float32)
    doc_ids = jnp.searchsorted(jnp.cumsum(uneven_parts(key_list[6], TOKENS // SEG, TOKENS, 2 * SEG, 1)), jnp.arange(TOKENS), side="right").astype(jnp.int32)
    return dict(tokens=tokens, w_qkv=w_qkv, w_pos=w_pos, w_out=w_out, content_bias=content_bias, position_bias=position_bias, doc_ids=doc_ids)


def sinus_table(count, width):
    place = jnp.arange(count, dtype=jnp.float32)[:, None]
    freqs = 1.0 / 10000.0 ** (jnp.arange(0, width, 2, dtype=jnp.float32) / width)
    angle = place * freqs[None, :]
    return jnp.concatenate([jnp.sin(angle), jnp.cos(angle)], axis=1).astype(jnp.bfloat16)

def attend(query_content, query_pos, keys, values, rel_keys, allowed, heads_here, head_dim):
    rows = query_content.shape[0]
    span = keys.shape[0]
    qc_heads = query_content.reshape(rows, heads_here, head_dim).astype(jnp.float32)
    qp_heads = query_pos.reshape(rows, heads_here, head_dim).astype(jnp.float32)
    key_heads = keys.reshape(span, heads_here, head_dim).astype(jnp.float32)
    val_heads = values.reshape(span, heads_here, head_dim).astype(jnp.float32)
    rel_heads = rel_keys.reshape(span, heads_here, head_dim).astype(jnp.float32)
    content = jnp.einsum('ihd,jhd->hij', qc_heads, key_heads)
    pos_full = jnp.einsum('ihd,rhd->hir', qp_heads, rel_heads)
    offset = jnp.arange(rows, dtype=jnp.int32)[:, None] + span // 2 - jnp.arange(span, dtype=jnp.int32)[None, :]
    offset = jnp.clip(offset, 0, span - 1)
    pos = jnp.take_along_axis(pos_full, jnp.broadcast_to(offset[None], pos_full.shape), axis=2)
    score = (content + pos) * (1.0 / jnp.sqrt(jnp.float32(head_dim)))
    score = jnp.where(allowed[None], score, jnp.float32(-1e+30))
    top = lax.optimization_barrier(jnp.max(score, axis=2, keepdims=True))
    expo = jnp.where(allowed[None], jnp.exp(score - top), jnp.float32(0.0))
    weights = (expo / lax.optimization_barrier(jnp.sum(expo, axis=2, keepdims=True))).astype(jnp.bfloat16)
    out = jnp.einsum('hij,jhd->ihd', weights.astype(jnp.float32), val_heads)
    return out.astype(jnp.bfloat16).reshape(rows, heads_here * head_dim)

def reference(tokens, w_qkv, w_pos, w_out, content_bias, position_bias, doc_ids):
    query = jnp.dot(tokens, w_qkv[0], preferred_element_type=jnp.float32)
    query_content = (query + content_bias.reshape(D)[None, :]).astype(jnp.bfloat16)
    query_pos = (query + position_bias.reshape(D)[None, :]).astype(jnp.bfloat16)
    key_rows = jnp.dot(tokens, w_qkv[1], preferred_element_type=jnp.float32).astype(jnp.bfloat16)
    value_rows = jnp.dot(tokens, w_qkv[2], preferred_element_type=jnp.float32).astype(jnp.bfloat16)
    rel_keys = jnp.dot(sinus_table(2 * SEG, D), w_pos, preferred_element_type=jnp.float32).astype(jnp.bfloat16)
    key_padded = jnp.concatenate([jnp.zeros((SEG, D), jnp.bfloat16), key_rows], axis=0)
    value_padded = jnp.concatenate([jnp.zeros((SEG, D), jnp.bfloat16), value_rows], axis=0)
    doc_padded = jnp.concatenate([jnp.full((SEG,), -1, jnp.int32), doc_ids.astype(jnp.int32)], axis=0)
    reach = jnp.arange(2 * SEG, dtype=jnp.int32)[None, :] <= jnp.arange(SEG, dtype=jnp.int32)[:, None] + SEG

    def one_segment(segment):
        start = (segment * SEG).astype(jnp.int32)
        keys = lax.dynamic_slice_in_dim(key_padded, start, 2 * SEG, 0)
        values = lax.dynamic_slice_in_dim(value_padded, start, 2 * SEG, 0)
        key_doc = lax.dynamic_slice_in_dim(doc_padded, start, 2 * SEG, 0)
        own_doc = lax.dynamic_slice_in_dim(doc_ids.astype(jnp.int32), start, SEG, 0)
        qc_rows = lax.dynamic_slice_in_dim(query_content, start, SEG, 0)
        qp_rows = lax.dynamic_slice_in_dim(query_pos, start, SEG, 0)
        allowed = reach & (key_doc[None, :] == own_doc[:, None])
        return attend(qc_rows, qp_rows, keys, values, rel_keys, allowed, HEADS, HEAD_DIM)
    head_out = lax.map(one_segment, jnp.arange(TOKENS // SEG, dtype=jnp.int32))
    head_out = head_out.reshape(TOKENS, D)
    return jnp.dot(head_out, w_out, preferred_element_type=jnp.float32).astype(jnp.bfloat16)
```

```python
import functools

import jax
import jax.numpy as jnp
from jax import lax
from jax.experimental import pallas as pl
from jax.experimental.pallas import tpu as pltpu
from jax.sharding import PartitionSpec as P

BF16 = jnp.bfloat16
F32 = jnp.float32
VMEM_LIMIT = 40 * 1024 * 1024


def vmem_spec():
    return pl.BlockSpec(memory_space=pltpu.VMEM)


def hbm_spec():
    return pl.BlockSpec(memory_space=pl.ANY)


def call(kernel, out_shape, in_specs, scratch, flops, nbytes, name, transcendentals=0):
    outs = jax.tree.map(lambda _: vmem_spec(), out_shape)
    return pl.pallas_call(
        kernel,
        out_shape=out_shape,
        in_specs=in_specs,
        out_specs=outs,
        scratch_shapes=scratch,
        compiler_params=pltpu.CompilerParams(vmem_limit_bytes=VMEM_LIMIT),
        cost_estimate=pl.CostEstimate(
            flops=flops, bytes_accessed=nbytes, transcendentals=transcendentals
        ),
        name=name,
    )


def dot(a, b):
    return jnp.dot(a, b, preferred_element_type=F32)


def dot_nt(a, b):
    return lax.dot_general(a, b, (((1,), (1,)), ((), ())), preferred_element_type=F32)


def rel_kernel(parts, w_ref, out_ref, wbuf, table, sems):
    rows, cols = out_ref.shape
    width = w_ref.shape[0]
    half = width // 2
    depth = width // parts

    def copy(i):
        return pltpu.make_async_copy(
            w_ref.at[pl.ds(i * depth, depth)], wbuf.at[pl.ds(i * depth, depth)], sems.at[i]
        )

    for i in range(parts):
        copy(i).start()
    fine = 16
    coarse = rows // fine
    index = lax.broadcasted_iota(jnp.int32, (1, half), 1).astype(F32) * 2.0
    freqs = 1.0 / 10000.0 ** (index / width)
    low = (fine - 1 - lax.broadcasted_iota(jnp.int32, (fine, half), 0)).astype(F32) * freqs
    high = (lax.broadcasted_iota(jnp.int32, (coarse, half), 0) * fine).astype(F32) * freqs
    sin_low, cos_low = jnp.sin(low), jnp.cos(low)
    sin_high, cos_high = jnp.sin(high), jnp.cos(high)
    for a in range(coarse):
        sh, ch = sin_high[a : a + 1], cos_high[a : a + 1]
        first = (coarse - 1 - a) * fine
        table[first : first + fine, :half] = (sh * cos_low + ch * sin_low).astype(BF16)
        table[first : first + fine, half:] = (ch * cos_low - sh * sin_low).astype(BF16)
    total = jnp.zeros((rows, cols), F32)
    for i in range(parts):
        copy(i).wait()
        total = total + dot(
            table[:, i * depth : (i + 1) * depth], wbuf[i * depth : (i + 1) * depth]
        )
    out_ref[...] = total.astype(BF16)


def rel_keys_reversed(w_pos, rows):
    width, cols = w_pos.shape
    parts = 8
    return call(
        functools.partial(rel_kernel, parts),
        jax.ShapeDtypeStruct((rows, cols), BF16),
        [hbm_spec()],
        [
            pltpu.VMEM((width, cols), BF16),
            pltpu.VMEM((rows, width), BF16),
            pltpu.SemaphoreType.DMA((parts,)),
        ],
        2 * rows * width * cols,
        2 * width * cols,
        "rel_keys",
        4 * 16 * width,
    )(w_pos)


def kv_kernel(first, last, place_ref, mine_ref, other_ref, w_ref, *refs):
    refs = list(refs)
    acc_ref = None if first else refs.pop(0)
    out_ref, wbuf, sems = refs
    depth = mine_ref.shape[1]
    rows = mine_ref.shape[0]

    def copy(i, c):
        start = pl.multiple_of(place_ref[i] * depth, depth)
        return pltpu.make_async_copy(
            w_ref.at[c + 1, pl.ds(start, depth)], wbuf.at[c, i], sems.at[c, i]
        )

    for c in range(2):
        for i in range(2):
            copy(i, c).start()
    for c in range(2):
        total = None if first else acc_ref[c]
        for i, x_ref in enumerate((mine_ref, other_ref)):
            copy(i, c).wait()
            term = dot(x_ref[...], wbuf[c, i])
            total = term if total is None else total + term
        out_ref[c] = total.astype(out_ref.dtype)


def kv_step(place, mine, other, w_qkv, acc, last):
    rows, depth = mine.shape
    cols = w_qkv.shape[2]
    first = acc is None
    args = [place, mine, other, w_qkv] + ([] if first else [acc])
    specs = [pl.BlockSpec(memory_space=pltpu.SMEM), vmem_spec(), vmem_spec(), hbm_spec()]
    specs += [] if first else [vmem_spec()]
    return call(
        functools.partial(kv_kernel, first, last),
        jax.ShapeDtypeStruct((2, rows, cols), BF16 if last else F32),
        specs,
        [pltpu.VMEM((2, 2, depth, cols), BF16), pltpu.SemaphoreType.DMA((2, 2))],
        8 * rows * depth * cols,
        8 * depth * cols,
        "kv_step",
    )(*args)


def q_kernel(count, place_ref, *refs):
    x_refs = refs[:count]
    w_ref, cb_ref, pb_ref, qc_ref, qp_ref, wbuf, sems = refs[count:]
    depth = x_refs[0].shape[1]

    def copy(i):
        start = pl.multiple_of(place_ref[i] * depth, depth)
        return pltpu.make_async_copy(w_ref.at[0, pl.ds(start, depth)], wbuf.at[i], sems.at[i])

    for i in range(count):
        copy(i).start()
    total = None
    for i in range(count):
        copy(i).wait()
        term = dot(x_refs[i][...], wbuf[i])
        total = term if total is None else total + term
    qc_ref[...] = (total + cb_ref[...]).astype(BF16)
    qp_ref[...] = (total + pb_ref[...]).astype(BF16)


def queries(places, chunks, w_qkv, content_bias, position_bias):
    count = len(chunks)
    rows, depth = chunks[0].shape
    cols = w_qkv.shape[2]
    out = jax.ShapeDtypeStruct((rows, cols), BF16)
    return call(
        functools.partial(q_kernel, count),
        (out, out),
        [pl.BlockSpec(memory_space=pltpu.SMEM)]
        + [vmem_spec()] * count
        + [hbm_spec(), vmem_spec(), vmem_spec()],
        [pltpu.VMEM((count, depth, cols), BF16), pltpu.SemaphoreType.DMA((count,))],
        2 * count * rows * depth * cols,
        2 * count * depth * cols,
        "queries",
    )(places, *chunks, w_qkv, content_bias.reshape(1, cols), position_bias.reshape(1, cols))


def attend_kernel(
    heads, blocks, place_ref, qc_ref, qp_ref, mem_ref, own_ref, rel_ref, qdoc_ref, kdoc_ref, w_ref,
    away_ref, keep_ref, wbuf, head_out, sems,
):
    rows = qc_ref.shape[0]
    head_dim = qc_ref.shape[1] // heads
    width = away_ref.shape[2]
    half = blocks // 2

    def copy(b):
        start = pl.multiple_of(place_ref[b] * width, width)
        return pltpu.make_async_copy(w_ref.at[:, pl.ds(start, width)], wbuf.at[b], sems.at[b])

    for b in range(blocks):
        copy(b).start()
    span = 2 * rows
    query = lax.broadcasted_iota(jnp.int32, (rows, span), 0)
    key = lax.broadcasted_iota(jnp.int32, (rows, span), 1)
    allowed = (key <= query + rows) & (kdoc_ref[...] == qdoc_ref[...])
    scale = 1.0 / (float(head_dim) ** 0.5)
    for h in range(heads):
        part = slice(h * head_dim, (h + 1) * head_dim)
        qc = qc_ref[:, part]
        content = jnp.concatenate(
            [dot_nt(qc, mem_ref[0, :, part]), dot_nt(qc, own_ref[0, :, part])], axis=1
        )
        pos = pltpu.roll(
            dot_nt(qp_ref[:, part], rel_ref[:, part]), rows + 1, 1, stride=1, stride_axis=0
        )
        score = jnp.where(allowed, (content + pos) * scale, -1e30)
        top = jnp.max(score, axis=1, keepdims=True)
        expo = jnp.where(allowed, jnp.exp(score - top), 0.0)
        weights = (expo / jnp.sum(expo, axis=1, keepdims=True)).astype(BF16)
        out = dot(weights[:, :rows], mem_ref[1, :, part])
        out = out + dot(weights[:, rows:], own_ref[1, :, part])
        head_out[:, part] = out.astype(BF16)
    for b in range(half):
        copy(b).wait()
        away_ref[b] = dot(head_out[...], wbuf[b]).astype(BF16)
    for b in range(half):
        copy(half + b).wait()
        keep_ref[b] = dot(head_out[...], wbuf[half + b])


def attend(places, query_content, query_pos, mem, own, rel, qdoc, kdoc, w_out, heads):
    rows, cols = query_content.shape
    blocks = places.shape[0]
    width = w_out.shape[1] // blocks
    half = blocks // 2
    return call(
        functools.partial(attend_kernel, heads, blocks),
        (
            jax.ShapeDtypeStruct((half, rows, width), BF16),
            jax.ShapeDtypeStruct((half, rows, width), F32),
        ),
        [pl.BlockSpec(memory_space=pltpu.SMEM)] + [vmem_spec()] * 7 + [hbm_spec()],
        [
            pltpu.VMEM((blocks, cols, width), BF16),
            pltpu.VMEM((rows, cols), BF16),
            pltpu.SemaphoreType.DMA((blocks,)),
        ],
        2 * rows * cols * w_out.shape[1] + 12 * rows * rows * cols,
        2 * cols * w_out.shape[1],
        "attend",
    )(places, query_content, query_pos, mem, own, rel, qdoc, kdoc, w_out)


def shards(tokens, w_qkv, w_pos, w_out, content_bias, position_bias, doc_ids):
    rows = tokens.shape[0]
    heads = content_bias.shape[0]
    count = lax.axis_size("mp")
    chips = count // 2
    segments = lax.axis_size("seq")
    me = lax.axis_index("mp")
    chip, core = me // 2, me % 2

    def across(value, k):
        return lax.ppermute(value, "mp", [(i, (i + 2 * k) % count) for i in range(count)])

    def swap(value):
        return lax.ppermute(value, "mp", [(i, i ^ 1) for i in range(count)])

    def onward(value):
        return lax.ppermute(value, "seq", [(i, i + 1) for i in range(segments - 1)])

    mine = [tokens] + [across(tokens, k) for k in range(1, chips)]
    other = [swap(chunk) for chunk in mine]
    mem_doc = onward(doc_ids)
    mem_doc = jnp.where(lax.axis_index("seq") > 0, mem_doc, -1)
    kdoc = jnp.concatenate([mem_doc, doc_ids]).reshape(1, 2 * rows)
    qdoc = doc_ids.reshape(rows, 1)
    rel = rel_keys_reversed(w_pos, 2 * rows)

    sources = [(chip - k) % chips for k in range(chips)]
    place = [jnp.stack([2 * s + core, 2 * s + 1 - core]) for s in sources]
    acc = None
    for k in range(chips):
        acc = kv_step(place[k], mine[k], other[k], w_qkv, acc, k == chips - 1)
    mem = onward(acc)
    query_content, query_pos = queries(
        jnp.concatenate(place),
        [chunk for pair in zip(mine, other) for chunk in pair],
        w_qkv,
        content_bias,
        position_bias,
    )
    targets = [(chip + k) % chips for k in range(chips)]
    columns = jnp.stack([2 * t + 1 - core for t in targets] + [2 * t + core for t in targets])
    away, keep = attend(
        columns, query_content, query_pos, mem, acc, rel, qdoc, kdoc, w_out, heads
    )
    total = keep + swap(away).astype(F32)
    result = total[0]
    for k in range(1, chips):
        result = result + across(total[k].astype(BF16), k).astype(F32)
    return result.astype(BF16)


def solution(mesh):
    in_specs = (
        P("seq", "mp"),
        P(None, None, "mp"),
        P(None, "mp"),
        P("mp", None),
        P("mp", None),
        P("mp", None),
        P("seq"),
    )
    out_specs = P("seq", "mp")
    return jax.shard_map(shards, mesh=mesh, in_specs=in_specs, out_specs=out_specs, check_vma=False)
```

```python
import functools

import jax
import jax.numpy as jnp
from jax import lax
from jax.experimental import pallas as pl
from jax.experimental.pallas import tpu as pltpu
from jax.sharding import PartitionSpec as P

BF16 = jnp.bfloat16
F32 = jnp.float32
VMEM_LIMIT = 24 * 1024 * 1024


def vmem_spec():
    return pl.BlockSpec(memory_space=pltpu.VMEM)


def hbm_spec():
    return pl.BlockSpec(memory_space=pl.ANY)


def in_hbm(value):
    return pltpu.with_memory_space_constraint(value, pltpu.HBM)


def call(kernel, out_shape, in_specs, scratch, flops, nbytes, name, transcendentals=0):
    outs = jax.tree.map(lambda _: vmem_spec(), out_shape)
    return pl.pallas_call(
        kernel,
        out_shape=out_shape,
        in_specs=in_specs,
        out_specs=outs,
        scratch_shapes=scratch,
        compiler_params=pltpu.CompilerParams(vmem_limit_bytes=VMEM_LIMIT),
        cost_estimate=pl.CostEstimate(
            flops=flops, bytes_accessed=nbytes, transcendentals=transcendentals
        ),
        name=name,
    )


def dot(a, b):
    return jnp.dot(a, b, preferred_element_type=F32)


def dot_nt(a, b):
    return lax.dot_general(a, b, (((1,), (1,)), ((), ())), preferred_element_type=F32)


def load_kernel(parts, w_pos, w_qkv, w_out, rel_ref, qkv_ref, out_ref, wbuf, table, sems):
    rows, cols = rel_ref.shape
    width = w_pos.shape[0]
    half = width // 2
    depth = width // parts

    def pos_copy(i):
        part = pl.ds(i * depth, depth)
        return pltpu.make_async_copy(w_pos.at[part], wbuf.at[part], sems.at[i])

    copies = [pos_copy(i) for i in range(parts)]
    for c in (1, 2, 0):
        copies.append(pltpu.make_async_copy(w_qkv.at[c], qkv_ref.at[c], sems.at[parts + c]))
    copies.append(pltpu.make_async_copy(w_out, out_ref, sems.at[parts + 3]))
    for item in copies:
        item.start()
    fine = 16
    coarse = rows // fine
    index = lax.broadcasted_iota(jnp.int32, (1, half), 1).astype(F32) * 2.0
    freqs = 1.0 / 10000.0 ** (index / width)
    low = (fine - 1 - lax.broadcasted_iota(jnp.int32, (fine, half), 0)).astype(F32) * freqs
    high = (lax.broadcasted_iota(jnp.int32, (coarse, half), 0) * fine).astype(F32) * freqs
    sin_low, cos_low = jnp.sin(low), jnp.cos(low)
    sin_high, cos_high = jnp.sin(high), jnp.cos(high)
    for a in range(coarse):
        sh, ch = sin_high[a : a + 1], cos_high[a : a + 1]
        first = (coarse - 1 - a) * fine
        table[first : first + fine, :half] = (sh * cos_low + ch * sin_low).astype(BF16)
        table[first : first + fine, half:] = (ch * cos_low - sh * sin_low).astype(BF16)
    total = jnp.zeros((rows, cols), F32)
    for i in range(parts):
        copies[i].wait()
        total = total + dot(
            table[:, i * depth : (i + 1) * depth], wbuf[i * depth : (i + 1) * depth]
        )
    rel_ref[...] = total.astype(BF16)
    for item in copies[parts:]:
        item.wait()


def load(w_pos, w_qkv, w_out, rows):
    width, cols = w_pos.shape
    parts = 8
    return call(
        functools.partial(load_kernel, parts),
        (
            pltpu.VMEM((rows, cols), BF16),
            pltpu.VMEM(w_qkv.shape, BF16),
            pltpu.VMEM(w_out.shape, BF16),
        ),
        [hbm_spec()] * 3,
        [
            pltpu.VMEM((width, cols), BF16),
            pltpu.VMEM((rows, width), BF16),
            pltpu.SemaphoreType.DMA((parts + 4,)),
        ],
        2 * rows * width * cols,
        20 * width * cols,
        "load",
        4 * 16 * width,
    )(in_hbm(w_pos), in_hbm(w_qkv), in_hbm(w_out))


def kv_kernel(first, last, back, mine_ref, other_ref, w_ref, *refs):
    refs = list(refs)
    acc_ref = None if first else refs.pop(0)
    doc_ref = refs.pop(0) if last else None
    (out_ref,) = refs
    rows, depth = mine_ref.shape
    core, place = here(back)
    for c in range(2):
        total = None if first else acc_ref[c]
        for i, x_ref in enumerate((mine_ref, other_ref)):
            start = pl.multiple_of(row_block(core, place, i) * depth, depth)
            term = dot(x_ref[...], w_ref[c + 1, pl.ds(start, depth)])
            total = term if total is None else total + term
        if last:
            out_ref[c * rows : (c + 1) * rows] = total.astype(BF16)
        else:
            out_ref[c] = total
    if last:
        out_ref[2 * rows :] = jnp.zeros((16, out_ref.shape[1]), BF16)
        out_ref[2 * rows :, :rows] = jnp.broadcast_to(doc_ref[...], (16, rows)).astype(BF16)


def here(back):
    me = lax.axis_index("mp")
    chips = lax.axis_size("mp") // 2
    return lax.rem(me, 2), lax.rem(me // 2 + chips - back, chips)


def row_block(core, place, i):
    return 2 * place + (core if i == 0 else 1 - core)


def kv_step(back, mine, other, w_qkv, acc, docs):
    rows, depth = mine.shape
    cols = w_qkv.shape[2]
    first, last = acc is None, docs is not None
    args = [mine, other, w_qkv] + ([] if first else [acc]) + ([docs] if last else [])
    out = pltpu.VMEM((2 * rows + 16, cols), BF16) if last else pltpu.VMEM((2, rows, cols), F32)
    return call(
        functools.partial(kv_kernel, first, last, back),
        out,
        [vmem_spec()] * len(args),
        [],
        8 * rows * depth * cols,
        8 * depth * cols,
        "kv_step",
    )(*args)


def q_kernel(count, *refs):
    x_refs = refs[:count]
    w_ref, cb_ref, pb_ref, qc_ref, qp_ref = refs[count:]
    depth = x_refs[0].shape[1]
    total = None
    for i in range(count):
        core, place = here(i // 2)
        start = pl.multiple_of(row_block(core, place, i % 2) * depth, depth)
        term = dot(x_refs[i][...], w_ref[0, pl.ds(start, depth)])
        total = term if total is None else total + term
    qc_ref[...] = (total + cb_ref[...]).astype(BF16)
    qp_ref[...] = (total + pb_ref[...]).astype(BF16)


def queries(chunks, w_qkv, content_bias, position_bias):
    count = len(chunks)
    rows, depth = chunks[0].shape
    cols = w_qkv.shape[2]
    out = pltpu.VMEM((rows, cols), BF16)
    return call(
        functools.partial(q_kernel, count),
        (out, out),
        [vmem_spec()] * (count + 3),
        [],
        2 * count * rows * depth * cols,
        2 * count * depth * cols,
        "queries",
    )(*chunks, w_qkv, content_bias.reshape(1, cols), position_bias.reshape(1, cols))


def attend_kernel(
    heads, qc_ref, qp_ref, mem_ref, own_ref, rel_ref, doc_ref, w_ref, away_ref, keep_ref, head_out
):
    rows = qc_ref.shape[0]
    head_dim = qc_ref.shape[1] // heads
    chips, _, width = away_ref.shape
    span = 2 * rows
    query = lax.broadcasted_iota(jnp.int32, (rows, span), 0)
    key = lax.broadcasted_iota(jnp.int32, (rows, span), 1)
    own_doc = jnp.broadcast_to(doc_ref[...], (rows, rows))
    mem_doc = jnp.broadcast_to(mem_ref[2 * rows : 2 * rows + 1, :rows].astype(F32), (rows, rows))
    query_doc = own_doc.T
    same = jnp.concatenate([mem_doc, own_doc], axis=1) == jnp.concatenate(
        [query_doc, query_doc], axis=1
    )
    allowed = (key <= query + rows) & same
    scale = 1.0 / (float(head_dim) ** 0.5)
    for h in range(heads):
        part = slice(h * head_dim, (h + 1) * head_dim)
        qc = qc_ref[:, part]
        content = jnp.concatenate(
            [dot_nt(qc, mem_ref[:rows, part]), dot_nt(qc, own_ref[:rows, part])], axis=1
        )
        pos = pltpu.roll(
            dot_nt(qp_ref[:, part], rel_ref[:, part]), rows + 1, 1, stride=1, stride_axis=0
        )
        score = jnp.where(allowed, (content + pos) * scale, -1e30)
        top = jnp.max(score, axis=1, keepdims=True)
        expo = jnp.where(allowed, jnp.exp(score - top), 0.0)
        weights = (expo / jnp.sum(expo, axis=1, keepdims=True)).astype(BF16)
        out = dot(weights[:, :rows], mem_ref[rows:span, part])
        out = out + dot(weights[:, rows:], own_ref[rows:span, part])
        head_out[:, part] = out.astype(BF16)
    core, chip = here(0)
    for away in (True, False):
        for k in range(chips):
            block = 2 * lax.rem(chip + k, chips) + (1 - core if away else core)
            start = pl.multiple_of(block * width, width)
            term = dot(head_out[...], w_ref[:, pl.ds(start, width)])
            if away:
                away_ref[k] = term.astype(BF16)
            else:
                keep_ref[k] = term


def attend(query_content, query_pos, mem, own, rel, docs, w_out, heads, count):
    rows, cols = query_content.shape
    width = w_out.shape[1] // count
    half = count // 2
    return call(
        functools.partial(attend_kernel, heads),
        (pltpu.VMEM((half, rows, width), BF16), pltpu.VMEM((half, rows, width), F32)),
        [vmem_spec()] * 7,
        [pltpu.VMEM((rows, cols), BF16)],
        2 * rows * cols * w_out.shape[1] + 12 * rows * rows * cols,
        2 * cols * w_out.shape[1],
        "attend",
    )(query_content, query_pos, mem, own, rel, docs, w_out)


def shards(tokens, w_qkv, w_pos, w_out, content_bias, position_bias, doc_ids):
    rows = tokens.shape[0]
    heads = content_bias.shape[0]
    count = lax.axis_size("mp")
    chips = count // 2
    segments = lax.axis_size("seq")

    def across(value, k):
        return lax.ppermute(value, "mp", [(i, (i + 2 * k) % count) for i in range(count)])

    def swap(value):
        return lax.ppermute(value, "mp", [(i, i ^ 1) for i in range(count)])

    def onward(value):
        return lax.ppermute(value, "seq", [(i, i + 1) for i in range(segments - 1)])

    mine = [tokens] + [across(tokens, k) for k in range(1, chips)]
    other = [swap(chunk) for chunk in mine]
    docs = (doc_ids + 1).astype(F32).reshape(1, rows)
    rel, w_qkv, w_out = load(w_pos, w_qkv, w_out, 2 * rows)
    own = None
    for k in range(chips):
        own = kv_step(k, mine[k], other[k], w_qkv, own, docs if k == chips - 1 else None)
    mem = onward(own)
    query_content, query_pos = queries(
        [chunk for pair in zip(mine, other) for chunk in pair], w_qkv, content_bias, position_bias
    )
    away, keep = attend(
        query_content, query_pos, mem, own, rel, docs, w_out, heads, count
    )
    total = keep + swap(away).astype(F32)
    result = total[0]
    for k in range(1, chips):
        result = result + across(total[k].astype(BF16), k).astype(F32)
    return result.astype(BF16)


def solution(mesh):
    in_specs = (
        P("seq", "mp"),
        P(None, None, "mp"),
        P(None, "mp"),
        P("mp", None),
        P("mp", None),
        P("mp", None),
        P("seq"),
    )
    out_specs = P("seq", "mp")
    return jax.shard_map(shards, mesh=mesh, in_specs=in_specs, out_specs=out_specs, check_vma=False)
```

```python
import functools

import jax
import jax.numpy as jnp
from jax import lax
from jax.experimental import pallas as pl
from jax.experimental.pallas import tpu as pltpu
from jax.sharding import PartitionSpec as P

BF16 = jnp.bfloat16
F32 = jnp.float32
VMEM_LIMIT = 24 * 1024 * 1024


def vmem_spec():
    return pl.BlockSpec(memory_space=pltpu.VMEM)


def hbm_spec():
    return pl.BlockSpec(memory_space=pl.ANY)


def in_hbm(value):
    return pltpu.with_memory_space_constraint(value, pltpu.HBM)


def call(kernel, out_shape, in_specs, scratch, flops, nbytes, name, transcendentals=0):
    outs = jax.tree.map(lambda _: vmem_spec(), out_shape)
    return pl.pallas_call(
        kernel,
        out_shape=out_shape,
        in_specs=in_specs,
        out_specs=outs,
        scratch_shapes=scratch,
        compiler_params=pltpu.CompilerParams(vmem_limit_bytes=VMEM_LIMIT),
        cost_estimate=pl.CostEstimate(
            flops=flops, bytes_accessed=nbytes, transcendentals=transcendentals
        ),
        name=name,
    )


def dot(a, b):
    return jnp.dot(a, b, preferred_element_type=F32)


def dot_nt(a, b):
    return lax.dot_general(a, b, (((1,), (1,)), ((), ())), preferred_element_type=F32)


def load_kernel(parts, w_pos, w_qkv, w_out, rel_ref, qkv_ref, out_ref, wbuf, table, sems):
    rows, cols = rel_ref.shape
    width = w_pos.shape[0]
    half = width // 2
    depth = width // parts

    def pos_copy(i):
        part = pl.ds(i * depth, depth)
        return pltpu.make_async_copy(w_pos.at[part], wbuf.at[part], sems.at[i])

    copies = [pos_copy(i) for i in range(parts)]
    for c in (1, 2, 0):
        copies.append(pltpu.make_async_copy(w_qkv.at[c], qkv_ref.at[c], sems.at[parts + c]))
    copies.append(pltpu.make_async_copy(w_out, out_ref, sems.at[parts + 3]))
    for item in copies:
        item.start()
    fine = 16
    coarse = rows // fine
    index = lax.broadcasted_iota(jnp.int32, (1, half), 1).astype(F32) * 2.0
    freqs = 1.0 / 10000.0 ** (index / width)
    low = (fine - 1 - lax.broadcasted_iota(jnp.int32, (fine, half), 0)).astype(F32) * freqs
    high = (lax.broadcasted_iota(jnp.int32, (coarse, half), 0) * fine).astype(F32) * freqs
    sin_low, cos_low = jnp.sin(low), jnp.cos(low)
    sin_high, cos_high = jnp.sin(high), jnp.cos(high)
    for a in range(coarse):
        sh, ch = sin_high[a : a + 1], cos_high[a : a + 1]
        first = (coarse - 1 - a) * fine
        table[first : first + fine, :half] = (sh * cos_low + ch * sin_low).astype(BF16)
        table[first : first + fine, half:] = (ch * cos_low - sh * sin_low).astype(BF16)
    total = jnp.zeros((rows, cols), F32)
    for i in range(parts):
        copies[i].wait()
        total = total + dot(
            table[:, i * depth : (i + 1) * depth], wbuf[i * depth : (i + 1) * depth]
        )
    rel_ref[...] = total.astype(BF16)
    for item in copies[parts:]:
        item.wait()


def load(w_pos, w_qkv, w_out, rows):
    width, cols = w_pos.shape
    parts = 8
    return call(
        functools.partial(load_kernel, parts),
        (
            pltpu.VMEM((rows, cols), BF16),
            pltpu.VMEM(w_qkv.shape, BF16),
            pltpu.VMEM(w_out.shape, BF16),
        ),
        [hbm_spec()] * 3,
        [
            pltpu.VMEM((width, cols), BF16),
            pltpu.VMEM((rows, width), BF16),
            pltpu.SemaphoreType.DMA((parts + 4,)),
        ],
        rows * width,
        rows * width,
        "load",
    )(in_hbm(w_pos), in_hbm(w_qkv), in_hbm(w_out))


def kv_kernel(first, last, back, mine_ref, other_ref, w_ref, *refs):
    refs = list(refs)
    acc_ref = None if first else refs.pop(0)
    doc_ref = refs.pop(0) if last else None
    (out_ref,) = refs
    rows, depth = mine_ref.shape
    core, place = here(back)
    for c in range(2):
        total = None if first else acc_ref[c]
        for i, x_ref in enumerate((mine_ref, other_ref)):
            start = pl.multiple_of(row_block(core, place, i) * depth, depth)
            term = dot(x_ref[...], w_ref[c + 1, pl.ds(start, depth)])
            total = term if total is None else total + term
        if last:
            out_ref[c * rows : (c + 1) * rows] = total.astype(BF16)
        else:
            out_ref[c] = total
    if last:
        out_ref[2 * rows :] = jnp.zeros((16, out_ref.shape[1]), BF16)
        out_ref[2 * rows :, :rows] = jnp.broadcast_to(doc_ref[...], (16, rows)).astype(BF16)


def here(back):
    me = lax.axis_index("mp")
    chips = lax.axis_size("mp") // 2
    return lax.rem(me, 2), lax.rem(me // 2 + chips - back, chips)


def row_block(core, place, i):
    return 2 * place + (core if i == 0 else 1 - core)


def kv_step(back, mine, other, w_qkv, acc, docs):
    rows, depth = mine.shape
    cols = w_qkv.shape[2]
    first, last = acc is None, docs is not None
    args = [mine, other, w_qkv] + ([] if first else [acc]) + ([docs] if last else [])
    out = pltpu.VMEM((2 * rows + 16, cols), BF16) if last else pltpu.VMEM((2, rows, cols), F32)
    return call(
        functools.partial(kv_kernel, first, last, back),
        out,
        [vmem_spec()] * len(args),
        [],
        rows * depth,
        rows * depth,
        "kv_step",
    )(*args)


def q_kernel(count, *refs):
    x_refs = refs[:count]
    w_ref, cb_ref, pb_ref, qc_ref, qp_ref = refs[count:]
    depth = x_refs[0].shape[1]
    total = None
    for i in range(count):
        core, place = here(i // 2)
        start = pl.multiple_of(row_block(core, place, i % 2) * depth, depth)
        term = dot(x_refs[i][...], w_ref[0, pl.ds(start, depth)])
        total = term if total is None else total + term
    qc_ref[...] = (total + cb_ref[...]).astype(BF16)
    qp_ref[...] = (total + pb_ref[...]).astype(BF16)


def queries(chunks, w_qkv, content_bias, position_bias):
    count = len(chunks)
    rows, depth = chunks[0].shape
    cols = w_qkv.shape[2]
    out = pltpu.VMEM((rows, cols), BF16)
    return call(
        functools.partial(q_kernel, count),
        (out, out),
        [vmem_spec()] * (count + 3),
        [],
        2 * count * rows * depth * cols,
        2 * count * depth * cols,
        "queries",
    )(*chunks, w_qkv, content_bias.reshape(1, cols), position_bias.reshape(1, cols))


def attend_kernel(
    heads, qc_ref, qp_ref, mem_ref, own_ref, rel_ref, doc_ref, w_ref, away_ref, keep_ref, head_out
):
    rows = qc_ref.shape[0]
    head_dim = qc_ref.shape[1] // heads
    chips, _, width = away_ref.shape
    span = 2 * rows
    query = lax.broadcasted_iota(jnp.int32, (rows, span), 0)
    key = lax.broadcasted_iota(jnp.int32, (rows, span), 1)
    own_doc = jnp.broadcast_to(doc_ref[...], (rows, rows))
    mem_doc = jnp.broadcast_to(mem_ref[2 * rows : 2 * rows + 1, :rows].astype(F32), (rows, rows))
    query_doc = own_doc.T
    same = jnp.concatenate([mem_doc, own_doc], axis=1) == jnp.concatenate(
        [query_doc, query_doc], axis=1
    )
    allowed = (key <= query + rows) & same
    scale = 1.0 / (float(head_dim) ** 0.5)
    for h in range(heads):
        part = slice(h * head_dim, (h + 1) * head_dim)
        qc = qc_ref[:, part]
        content = jnp.concatenate(
            [dot_nt(qc, mem_ref[:rows, part]), dot_nt(qc, own_ref[:rows, part])], axis=1
        )
        pos = pltpu.roll(
            dot_nt(qp_ref[:, part], rel_ref[:, part]), rows + 1, 1, stride=1, stride_axis=0
        )
        score = jnp.where(allowed, (content + pos) * scale, -1e30)
        top = jnp.max(score, axis=1, keepdims=True)
        expo = jnp.where(allowed, jnp.exp(score - top), 0.0)
        weights = (expo / jnp.sum(expo, axis=1, keepdims=True)).astype(BF16)
        out = dot(weights[:, :rows], mem_ref[rows:span, part])
        out = out + dot(weights[:, rows:], own_ref[rows:span, part])
        head_out[:, part] = out.astype(BF16)
    core, chip = here(0)
    for away in (True, False):
        for k in range(chips):
            block = 2 * lax.rem(chip + k, chips) + (1 - core if away else core)
            start = pl.multiple_of(block * width, width)
            term = dot(head_out[...], w_ref[:, pl.ds(start, width)])
            if away:
                away_ref[k] = term.astype(BF16)
            else:
                keep_ref[k] = term


def attend(query_content, query_pos, mem, own, rel, docs, w_out, heads, count):
    rows, cols = query_content.shape
    width = w_out.shape[1] // count
    half = count // 2
    return call(
        functools.partial(attend_kernel, heads),
        (pltpu.VMEM((half, rows, width), BF16), pltpu.VMEM((half, rows, width), F32)),
        [vmem_spec()] * 7,
        [pltpu.VMEM((rows, cols), BF16)],
        2 * rows * cols * w_out.shape[1] + 12 * rows * rows * cols,
        2 * cols * w_out.shape[1],
        "attend",
    )(query_content, query_pos, mem, own, rel, docs, w_out)


def shards(tokens, w_qkv, w_pos, w_out, content_bias, position_bias, doc_ids):
    rows = tokens.shape[0]
    heads = content_bias.shape[0]
    count = lax.axis_size("mp")
    chips = count // 2
    segments = lax.axis_size("seq")

    def across(value, k):
        return lax.ppermute(value, "mp", [(i, (i + 2 * k) % count) for i in range(count)])

    def swap(value):
        return lax.ppermute(value, "mp", [(i, i ^ 1) for i in range(count)])

    def onward(value):
        return lax.ppermute(value, "seq", [(i, i + 1) for i in range(segments - 1)])

    mine = [tokens] + [across(tokens, k) for k in range(1, chips)]
    other = [swap(tokens)]
    docs = (doc_ids + 1).astype(F32).reshape(1, rows)
    rel, w_qkv, w_out = load(w_pos, w_qkv, w_out, 2 * rows)
    for k in range(1, chips):
        mine[k], rel = lax.optimization_barrier((mine[k], rel))
        other.append(swap(mine[k]))
    own = None
    for k in range(chips):
        own = kv_step(k, mine[k], other[k], w_qkv, own, docs if k == chips - 1 else None)
    mem = onward(own)
    query_content, query_pos = queries(
        [chunk for pair in zip(mine, other) for chunk in pair], w_qkv, content_bias, position_bias
    )
    away, keep = attend(
        query_content, query_pos, mem, own, rel, docs, w_out, heads, count
    )
    total = keep + swap(away).astype(F32)
    result = total[0]
    for k in range(1, chips):
        result = result + across(total[k].astype(BF16), k).astype(F32)
    return result.astype(BF16)


def solution(mesh):
    in_specs = (
        P("seq", "mp"),
        P(None, None, "mp"),
        P(None, "mp"),
        P("mp", None),
        P("mp", None),
        P("mp", None),
        P("seq"),
    )
    out_specs = P("seq", "mp")
    return jax.shard_map(shards, mesh=mesh, in_specs=in_specs, out_specs=out_specs, check_vma=False)
```

```python
import functools

import jax
import jax.numpy as jnp
from jax import lax
from jax.experimental import pallas as pl
from jax.experimental.pallas import tpu as pltpu
from jax.sharding import PartitionSpec as P

BF16 = jnp.bfloat16
F32 = jnp.float32
VMEM_LIMIT = 24 * 1024 * 1024


def vmem_spec():
    return pl.BlockSpec(memory_space=pltpu.VMEM)


def hbm_spec():
    return pl.BlockSpec(memory_space=pl.ANY)


def in_hbm(value):
    return pltpu.with_memory_space_constraint(value, pltpu.HBM)


def call(kernel, out_shape, in_specs, scratch, flops, nbytes, name, transcendentals=0):
    outs = jax.tree.map(lambda _: vmem_spec(), out_shape)
    return pl.pallas_call(
        kernel,
        out_shape=out_shape,
        in_specs=in_specs,
        out_specs=outs,
        scratch_shapes=scratch,
        compiler_params=pltpu.CompilerParams(vmem_limit_bytes=VMEM_LIMIT),
        cost_estimate=pl.CostEstimate(
            flops=flops, bytes_accessed=nbytes, transcendentals=transcendentals
        ),
        name=name,
    )


def dot(a, b):
    return jnp.dot(a, b, preferred_element_type=F32)


def dot_nt(a, b):
    return lax.dot_general(a, b, (((1,), (1,)), ((), ())), preferred_element_type=F32)


def load_kernel(parts, w_pos, w_qkv, w_out, rel_ref, qkv_ref, out_ref, wbuf, table, sems):
    rows, cols = rel_ref.shape
    width = w_pos.shape[0]
    half = width // 2
    depth = width // parts

    def pos_copy(i):
        part = pl.ds(i * depth, depth)
        return pltpu.make_async_copy(w_pos.at[part], wbuf.at[part], sems.at[i])

    copies = [pos_copy(i) for i in range(parts)]
    for c in (1, 2, 0):
        copies.append(pltpu.make_async_copy(w_qkv.at[c], qkv_ref.at[c], sems.at[parts + c]))
    copies.append(pltpu.make_async_copy(w_out, out_ref, sems.at[parts + 3]))
    for item in copies:
        item.start()
    fine = 16
    coarse = rows // fine
    index = lax.broadcasted_iota(jnp.int32, (1, half), 1).astype(F32) * 2.0
    freqs = 1.0 / 10000.0 ** (index / width)
    low = (fine - 1 - lax.broadcasted_iota(jnp.int32, (fine, half), 0)).astype(F32) * freqs
    high = (lax.broadcasted_iota(jnp.int32, (coarse, half), 0) * fine).astype(F32) * freqs
    sin_low, cos_low = jnp.sin(low), jnp.cos(low)
    sin_high, cos_high = jnp.sin(high), jnp.cos(high)
    for a in range(coarse):
        sh, ch = sin_high[a : a + 1], cos_high[a : a + 1]
        first = (coarse - 1 - a) * fine
        table[first : first + fine, :half] = (sh * cos_low + ch * sin_low).astype(BF16)
        table[first : first + fine, half:] = (ch * cos_low - sh * sin_low).astype(BF16)
    total = jnp.zeros((rows, cols), F32)
    for i in range(parts):
        copies[i].wait()
        total = total + dot(
            table[:, i * depth : (i + 1) * depth], wbuf[i * depth : (i + 1) * depth]
        )
    rel_ref[...] = total.astype(BF16)
    for item in copies[parts:]:
        item.wait()


def load(w_pos, w_qkv, w_out, rows):
    width, cols = w_pos.shape
    parts = 8
    return call(
        functools.partial(load_kernel, parts),
        (
            pltpu.VMEM((rows, cols), BF16),
            pltpu.VMEM(w_qkv.shape, BF16),
            pltpu.VMEM(w_out.shape, BF16),
        ),
        [hbm_spec()] * 3,
        [
            pltpu.VMEM((width, cols), BF16),
            pltpu.VMEM((rows, width), BF16),
            pltpu.SemaphoreType.DMA((parts + 4,)),
        ],
        rows * width,
        rows * width,
        "load",
    )(in_hbm(w_pos), in_hbm(w_qkv), in_hbm(w_out))


def here(back):
    me = lax.axis_index("mp")
    chips = lax.axis_size("mp") // 2
    return lax.rem(me, 2), lax.rem(me // 2 + chips - back, chips)


def row_block(core, place, i):
    return 2 * place + (core if i == 0 else 1 - core)


def kv_kernel(first, last, back, mine_ref, other_ref, w_ref, *refs):
    refs = list(refs)
    acc_ref = None if first else refs.pop(0)
    doc_ref = refs.pop(0) if last else None
    rows, depth = mine_ref.shape
    core, place = here(back)
    for c in range(2):
        total = None if first else acc_ref[c]
        for i, x_ref in enumerate((mine_ref, other_ref)):
            start = pl.multiple_of(row_block(core, place, i) * depth, depth)
            term = dot(x_ref[...], w_ref[c + 1, pl.ds(start, depth)])
            total = term if total is None else total + term
        if last:
            refs[c][:rows] = total.astype(BF16)
        else:
            refs[0][c] = total
    if last:
        key_ref = refs[0]
        key_ref[rows:] = jnp.zeros((16, key_ref.shape[1]), BF16)
        key_ref[rows:, :rows] = jnp.broadcast_to(doc_ref[...], (16, rows)).astype(BF16)


def kv_step(back, mine, other, w_qkv, acc, docs):
    rows, depth = mine.shape
    cols = w_qkv.shape[2]
    first, last = acc is None, docs is not None
    args = [mine, other, w_qkv] + ([] if first else [acc]) + ([docs] if last else [])
    out = pltpu.VMEM((2, rows, cols), F32)
    if last:
        out = (pltpu.VMEM((rows + 16, cols), BF16), pltpu.VMEM((rows, cols), BF16))
    return call(
        functools.partial(kv_kernel, first, last, back),
        out,
        [vmem_spec()] * len(args),
        [],
        rows * depth,
        rows * depth,
        "kv_step",
    )(*args)


def q_kernel(count, heads, *refs):
    x_refs = refs[:count]
    w_ref, cb_ref, pb_ref, key_ref, rel_ref, doc_ref, qc_ref, score_ref = refs[count:]
    rows, depth = x_refs[0].shape
    head_dim = qc_ref.shape[1] // heads
    total = None
    for i in range(count):
        core, place = here(i // 2)
        start = pl.multiple_of(row_block(core, place, i % 2) * depth, depth)
        term = dot(x_refs[i][...], w_ref[0, pl.ds(start, depth)])
        total = term if total is None else total + term
    query_content = (total + cb_ref[...]).astype(BF16)
    query_pos = (total + pb_ref[...]).astype(BF16)
    qc_ref[...] = query_content
    query = lax.broadcasted_iota(jnp.int32, (rows, rows), 0)
    key = lax.broadcasted_iota(jnp.int32, (rows, rows), 1)
    own_doc = jnp.broadcast_to(doc_ref[...], (rows, rows))
    allowed = (key <= query) & (own_doc == own_doc.T)
    scale = 1.0 / (float(head_dim) ** 0.5)
    for h in range(heads):
        part = slice(h * head_dim, (h + 1) * head_dim)
        pos = pltpu.roll(
            dot_nt(query_pos[:, part], rel_ref[:, part]), rows + 1, 1, stride=1, stride_axis=0
        )
        content = dot_nt(query_content[:, part], key_ref[:rows, part])
        score_ref[h, :, :rows] = pos[:, :rows]
        score_ref[h, :, rows:] = jnp.where(allowed, (content + pos[:, rows:]) * scale, -1e30)


def queries(chunks, w_qkv, content_bias, position_bias, own_key, rel, docs):
    count = len(chunks)
    rows, depth = chunks[0].shape
    cols = w_qkv.shape[2]
    heads = content_bias.shape[0]
    return call(
        functools.partial(q_kernel, count, heads),
        (pltpu.VMEM((rows, cols), BF16), pltpu.VMEM((heads, rows, 2 * rows), F32)),
        [vmem_spec()] * (count + 6),
        [],
        2 * count * rows * depth * cols,
        2 * count * depth * cols,
        "queries",
    )(
        *chunks,
        w_qkv,
        content_bias.reshape(1, cols),
        position_bias.reshape(1, cols),
        own_key,
        rel,
        docs,
    )


def weigh_kernel(qc_ref, score_ref, mem_ref, val_ref, doc_ref, weight_ref, out_ref):
    heads, rows, _ = score_ref.shape
    head_dim = qc_ref.shape[1] // heads
    exists = jnp.minimum(lax.axis_index("seq"), 1).astype(F32)
    mem_doc = jnp.broadcast_to(mem_ref[rows : rows + 1, :rows].astype(F32) * exists, (rows, rows))
    allowed = mem_doc == jnp.broadcast_to(doc_ref[...], (rows, rows)).T
    scale = 1.0 / (float(head_dim) ** 0.5)
    for h in range(heads):
        part = slice(h * head_dim, (h + 1) * head_dim)
        content = dot_nt(qc_ref[:, part], mem_ref[:rows, part])
        mem = jnp.where(allowed, (content + score_ref[h, :, :rows]) * scale, -1e30)
        own = score_ref[h, :, rows:]
        top = jnp.maximum(
            jnp.max(mem, axis=1, keepdims=True), jnp.max(own, axis=1, keepdims=True)
        )
        mem = jnp.where(mem > -1e29, jnp.exp(mem - top), 0.0)
        own = jnp.where(own > -1e29, jnp.exp(own - top), 0.0)
        total = jnp.sum(mem, axis=1, keepdims=True) + jnp.sum(own, axis=1, keepdims=True)
        weight_ref[h] = (mem / total).astype(BF16)
        out_ref[:, part] = dot((own / total).astype(BF16), val_ref[:, part])


def weigh(query_content, score, mem_key, own_val, docs):
    rows, cols = query_content.shape
    heads = score.shape[0]
    return call(
        weigh_kernel,
        (pltpu.VMEM((heads, rows, rows), BF16), pltpu.VMEM((rows, cols), F32)),
        [vmem_spec()] * 5,
        [],
        8 * rows * rows * cols,
        8 * rows * cols,
        "weigh",
    )(query_content, score, mem_key, own_val, docs)


def blocks_out(offsets, head_out, w_ref, away_ref, keep_ref):
    width = away_ref.shape[2]
    core, chip = here(0)
    chips = lax.axis_size("mp") // 2
    for away in (True, False):
        for i, k in enumerate(offsets):
            block = 2 * lax.rem(chip + k, chips) + (1 - core if away else core)
            start = pl.multiple_of(block * width, width)
            term = dot(head_out, w_ref[:, pl.ds(start, width)])
            if away:
                away_ref[i] = term.astype(BF16)
            else:
                keep_ref[i] = term


def mix_kernel(offsets, weight_ref, out_ref, mem_ref, w_ref, head_ref, away_ref, keep_ref):
    heads, rows, _ = weight_ref.shape
    head_dim = out_ref.shape[1] // heads
    for h in range(heads):
        part = slice(h * head_dim, (h + 1) * head_dim)
        out = out_ref[:, part] + dot(weight_ref[h], mem_ref[:, part])
        head_ref[:, part] = out.astype(BF16)
    blocks_out(offsets, head_ref[...], w_ref, away_ref, keep_ref)


def rest_kernel(offsets, head_ref, w_ref, away_ref, keep_ref):
    blocks_out(offsets, head_ref[...], w_ref, away_ref, keep_ref)


def block_shapes(offsets, rows, width):
    count = len(offsets)
    return (pltpu.VMEM((count, rows, width), BF16), pltpu.VMEM((count, rows, width), F32))


def mix(offsets, weights, out, mem_val, w_out, width):
    rows, cols = out.shape
    return call(
        functools.partial(mix_kernel, offsets),
        (pltpu.VMEM((rows, cols), BF16),) + block_shapes(offsets, rows, width),
        [vmem_spec()] * 4,
        [],
        4 * rows * cols * width * len(offsets),
        4 * cols * width * len(offsets),
        "mix",
    )(weights, out, mem_val, w_out)


def rest(offsets, head_out, w_out, width):
    rows, cols = head_out.shape
    return call(
        functools.partial(rest_kernel, offsets),
        block_shapes(offsets, rows, width),
        [vmem_spec()] * 2,
        [],
        4 * rows * cols * width * len(offsets),
        4 * cols * width * len(offsets),
        "rest",
    )(head_out, w_out)


def shards(tokens, w_qkv, w_pos, w_out, content_bias, position_bias, doc_ids):
    rows = tokens.shape[0]
    count = lax.axis_size("mp")
    chips = count // 2
    segments = lax.axis_size("seq")
    width = w_out.shape[1] // count

    def across(value, k):
        return lax.ppermute(value, "mp", [(i, (i + 2 * k) % count) for i in range(count)])

    def swap(value):
        return lax.ppermute(value, "mp", [(i, i ^ 1) for i in range(count)])

    def onward(value):
        return lax.ppermute(value, "seq", [(i, (i + 1) % segments) for i in range(segments)])

    mine = [tokens] + [across(tokens, k) for k in range(1, chips)]
    other = [swap(tokens)]
    docs = (doc_ids + 1).astype(F32).reshape(1, rows)
    rel, w_qkv, w_out = load(w_pos, w_qkv, w_out, 2 * rows)
    for k in range(1, chips):
        mine[k], rel = lax.optimization_barrier((mine[k], rel))
        other.append(swap(mine[k]))
    acc = None
    for k in range(chips):
        acc = kv_step(k, mine[k], other[k], w_qkv, acc, docs if k == chips - 1 else None)
    own_key, own_val = acc
    mem_key, mem_val = onward(own_key), onward(own_val)
    query_content, score = queries(
        [chunk for pair in zip(mine, other) for chunk in pair],
        w_qkv,
        content_bias,
        position_bias,
        own_key,
        rel,
        docs,
    )
    weights, out = weigh(query_content, score, mem_key, own_val, docs)
    first = [chips // 2]
    others = [k for k in range(chips) if k not in first]
    head_out, away, keep = mix(first, weights, out, mem_val, w_out, width)
    total = {first[0]: keep[0] + swap(away)[0].astype(F32)}
    away, keep = rest(others, head_out, w_out, width)
    away = swap(away).astype(F32)
    for i, k in enumerate(others):
        total[k] = keep[i] + away[i]
    result = total[0]
    for k in first + others:
        if k > 0:
            result = result + across(total[k].astype(BF16), k).astype(F32)
    return result.astype(BF16)


def solution(mesh):
    in_specs = (
        P("seq", "mp"),
        P(None, None, "mp"),
        P(None, "mp"),
        P("mp", None),
        P("mp", None),
        P("mp", None),
        P("seq"),
    )
    out_specs = P("seq", "mp")
    return jax.shard_map(shards, mesh=mesh, in_specs=in_specs, out_specs=out_specs, check_vma=False)
```

```python
import functools

import jax
import jax.numpy as jnp
from jax import lax
from jax.experimental import pallas as pl
from jax.experimental.pallas import tpu as pltpu
from jax.sharding import PartitionSpec as P

BF16 = jnp.bfloat16
F32 = jnp.float32
VMEM_LIMIT = 24 * 1024 * 1024


def vmem_spec():
    return pl.BlockSpec(memory_space=pltpu.VMEM)


def hbm_spec():
    return pl.BlockSpec(memory_space=pl.ANY)


def in_hbm(value):
    return pltpu.with_memory_space_constraint(value, pltpu.HBM)


def call(kernel, out_shape, in_specs, scratch, flops, nbytes, name, transcendentals=0):
    outs = jax.tree.map(lambda _: vmem_spec(), out_shape)
    return pl.pallas_call(
        kernel,
        out_shape=out_shape,
        in_specs=in_specs,
        out_specs=outs,
        scratch_shapes=scratch,
        compiler_params=pltpu.CompilerParams(vmem_limit_bytes=VMEM_LIMIT),
        cost_estimate=pl.CostEstimate(
            flops=flops, bytes_accessed=nbytes, transcendentals=transcendentals
        ),
        name=name,
    )


def dot(a, b):
    return jnp.dot(a, b, preferred_element_type=F32)


def dot_nt(a, b):
    return lax.dot_general(a, b, (((1,), (1,)), ((), ())), preferred_element_type=F32)


def load_kernel(parts, w_pos, w_qkv, rel_ref, kv_ref, wbuf, table, sems):
    rows, cols = rel_ref.shape
    width = w_pos.shape[0]
    half = width // 2
    depth = width // parts

    def pos_copy(i):
        part = pl.ds(i * depth, depth)
        return pltpu.make_async_copy(w_pos.at[part], wbuf.at[part], sems.at[i])

    copies = [pos_copy(i) for i in range(parts)]
    for c in range(2):
        copies.append(pltpu.make_async_copy(w_qkv.at[c + 1], kv_ref.at[c], sems.at[parts + c]))
    for item in copies:
        item.start()
    fine = 16
    coarse = rows // fine
    index = lax.broadcasted_iota(jnp.int32, (1, half), 1).astype(F32) * 2.0
    freqs = 1.0 / 10000.0 ** (index / width)
    low = (fine - 1 - lax.broadcasted_iota(jnp.int32, (fine, half), 0)).astype(F32) * freqs
    high = (lax.broadcasted_iota(jnp.int32, (coarse, half), 0) * fine).astype(F32) * freqs
    sin_low, cos_low = jnp.sin(low), jnp.cos(low)
    sin_high, cos_high = jnp.sin(high), jnp.cos(high)
    for a in range(coarse):
        sh, ch = sin_high[a : a + 1], cos_high[a : a + 1]
        first = (coarse - 1 - a) * fine
        table[first : first + fine, :half] = (sh * cos_low + ch * sin_low).astype(BF16)
        table[first : first + fine, half:] = (ch * cos_low - sh * sin_low).astype(BF16)
    total = jnp.zeros((rows, cols), F32)
    for i in range(parts):
        copies[i].wait()
        total = total + dot(
            table[:, i * depth : (i + 1) * depth], wbuf[i * depth : (i + 1) * depth]
        )
    rel_ref[...] = total.astype(BF16)
    for item in copies[parts:]:
        item.wait()


def load(w_pos, w_qkv, rows):
    width, cols = w_pos.shape
    parts = 8
    return call(
        functools.partial(load_kernel, parts),
        (pltpu.VMEM((rows, cols), BF16), pltpu.VMEM((2, width, cols), BF16)),
        [hbm_spec()] * 2,
        [
            pltpu.VMEM((width, cols), BF16),
            pltpu.VMEM((rows, width), BF16),
            pltpu.SemaphoreType.DMA((parts + 2,)),
        ],
        rows * width,
        rows * width,
        "load",
    )(in_hbm(w_pos), in_hbm(w_qkv))


def here(back):
    me = lax.axis_index("mp")
    chips = lax.axis_size("mp") // 2
    return lax.rem(me, 2), lax.rem(me // 2 + chips - back, chips)


def row_block(core, place, i):
    return 2 * place + (core if i == 0 else 1 - core)


def kv_kernel(sources, kinds, first, last, *refs):
    refs = list(refs)
    x_refs = [refs.pop(0) for _ in sources]
    w_ref = refs.pop(0)
    acc_ref = None if first else refs.pop(0)
    doc_ref = refs.pop(0) if last == "keys" else None
    (out_ref,) = refs
    rows, depth = x_refs[0].shape
    for kind in kinds:
        total = None if first else acc_ref[kind - 1]
        for (back, i), x_ref in zip(sources, x_refs):
            core, place = here(back)
            start = pl.multiple_of(row_block(core, place, i) * depth, depth)
            term = dot(x_ref[...], w_ref[kind - 1, pl.ds(start, depth)])
            total = term if total is None else total + term
        if last == "keys":
            head_dim = out_ref.shape[1]
            for h in range(total.shape[1] // head_dim):
                part = total[:, h * head_dim : (h + 1) * head_dim]
                out_ref[h * rows : (h + 1) * rows] = part.astype(BF16)
            docs = jnp.broadcast_to(doc_ref[...], (16, rows)).astype(BF16)
            out_ref[out_ref.shape[0] - 16 :] = docs
        elif last == "values":
            out_ref[...] = total.astype(BF16)
        else:
            out_ref[kind - 1] = total


def kv_step(chunks, w_qkv, acc, kinds=(1, 2), last=None, docs=None, heads=None):
    sources = tuple(chunks)
    rows, depth = chunks[sources[0]].shape
    cols = w_qkv.shape[2]
    args = [chunks[source] for source in sources] + [w_qkv]
    args += ([] if acc is None else [acc]) + ([] if docs is None else [docs])
    out = pltpu.VMEM((2, rows, cols), F32)
    if last == "keys":
        assert rows == cols // heads
        out = pltpu.VMEM((heads * rows + 16, cols // heads), BF16)
    elif last == "values":
        out = pltpu.VMEM((rows, cols), BF16)
    return call(
        functools.partial(kv_kernel, sources, kinds, acc is None, last),
        out,
        [vmem_spec()] * len(args),
        [],
        16 * rows * depth * cols,
        0,
        "kv_step",
    )(*args)


def q_kernel(count, heads, *refs):
    x_refs = refs[:count]
    w_ref, w_out, cb_ref, pb_ref, key_ref, rel_ref, doc_ref = refs[count : count + 7]
    qc_ref, score_ref, w_out_ref, wbuf, sems = refs[count + 7 :]
    rows, depth = x_refs[0].shape
    head_dim = qc_ref.shape[1] // heads

    def copy(i):
        core, place = here(i // 2)
        start = pl.multiple_of(row_block(core, place, i % 2) * depth, depth)
        return pltpu.make_async_copy(w_ref.at[0, pl.ds(start, depth)], wbuf.at[i], sems.at[i])

    copies = [copy(i) for i in range(count)]
    copies.append(pltpu.make_async_copy(w_out, w_out_ref, sems.at[count]))
    for item in copies:
        item.start()
    total = None
    for i in range(count):
        copies[i].wait()
        term = dot(x_refs[i][...], wbuf[i])
        total = term if total is None else total + term
    query_content = (total + cb_ref[...]).astype(BF16)
    query_pos = (total + pb_ref[...]).astype(BF16)
    qc_ref[...] = query_content
    query = lax.broadcasted_iota(jnp.int32, (rows, rows), 0)
    key = lax.broadcasted_iota(jnp.int32, (rows, rows), 1)
    own_doc = jnp.broadcast_to(doc_ref[...], (rows, rows))
    allowed = (key <= query) & (own_doc == own_doc.T)
    scale = 1.0 / (float(head_dim) ** 0.5)
    for h in range(heads):
        part = slice(h * head_dim, (h + 1) * head_dim)
        pos = pltpu.roll(
            dot_nt(query_pos[:, part], rel_ref[:, part]), rows + 1, 1, stride=1, stride_axis=0
        )
        content = dot_nt(query_content[:, part], key_ref[h * rows : (h + 1) * rows])
        score_ref[h, :, :rows] = pos[:, :rows]
        score_ref[h, :, rows:] = jnp.where(allowed, (content + pos[:, rows:]) * scale, -1e30)
    copies[count].wait()


def queries(chunks, w_qkv, w_out, content_bias, position_bias, own_key, rel, docs):
    count = len(chunks)
    rows, depth = chunks[0].shape
    cols = w_qkv.shape[2]
    heads = content_bias.shape[0]
    return call(
        functools.partial(q_kernel, count, heads),
        (
            pltpu.VMEM((rows, cols), BF16),
            pltpu.VMEM((heads, rows, 2 * rows), F32),
            pltpu.VMEM(w_out.shape, BF16),
        ),
        [vmem_spec()] * count + [hbm_spec()] * 2 + [vmem_spec()] * 5,
        [pltpu.VMEM((count, depth, cols), BF16), pltpu.SemaphoreType.DMA((count + 1,))],
        2 * count * rows * depth * cols,
        2 * count * depth * cols,
        "queries",
    )(
        *chunks,
        in_hbm(w_qkv),
        in_hbm(w_out),
        content_bias.reshape(1, cols),
        position_bias.reshape(1, cols),
        own_key,
        rel,
        docs,
    )


def weigh_kernel(qc_ref, score_ref, mem_ref, val_ref, doc_ref, weight_ref, out_ref):
    heads, rows, _ = score_ref.shape
    head_dim = qc_ref.shape[1] // heads
    exists = jnp.minimum(lax.axis_index("seq"), 1).astype(F32)
    mem_doc = mem_ref[heads * rows : heads * rows + 1].astype(F32) * exists
    mem_doc = jnp.broadcast_to(mem_doc, (rows, rows))
    allowed = mem_doc == jnp.broadcast_to(doc_ref[...], (rows, rows)).T
    scale = 1.0 / (float(head_dim) ** 0.5)
    for h in range(heads):
        part = slice(h * head_dim, (h + 1) * head_dim)
        content = dot_nt(qc_ref[:, part], mem_ref[h * rows : (h + 1) * rows])
        mem = jnp.where(allowed, (content + score_ref[h, :, :rows]) * scale, -1e30)
        own = score_ref[h, :, rows:]
        top = jnp.maximum(
            jnp.max(mem, axis=1, keepdims=True), jnp.max(own, axis=1, keepdims=True)
        )
        mem = jnp.where(mem > -1e29, jnp.exp(mem - top), 0.0)
        own = jnp.where(own > -1e29, jnp.exp(own - top), 0.0)
        total = jnp.sum(mem, axis=1, keepdims=True) + jnp.sum(own, axis=1, keepdims=True)
        weight_ref[h] = (mem / total).astype(BF16)
        out_ref[:, part] = dot((own / total).astype(BF16), val_ref[:, part])


def weigh(query_content, score, mem_key, own_val, docs):
    rows, cols = query_content.shape
    heads = score.shape[0]
    return call(
        weigh_kernel,
        (pltpu.VMEM((heads, rows, rows), BF16), pltpu.VMEM((rows, cols), F32)),
        [vmem_spec()] * 5,
        [],
        8 * rows * rows * cols,
        8 * rows * cols,
        "weigh",
    )(query_content, score, mem_key, own_val, docs)


def blocks_out(offsets, head_out, w_ref, away_ref, keep_ref):
    width = away_ref.shape[2]
    core, chip = here(0)
    chips = lax.axis_size("mp") // 2
    for away in (True, False):
        for i, k in enumerate(offsets):
            block = 2 * lax.rem(chip + k, chips) + (1 - core if away else core)
            start = pl.multiple_of(block * width, width)
            term = dot(head_out, w_ref[:, pl.ds(start, width)])
            if away:
                away_ref[i] = term.astype(BF16)
            else:
                keep_ref[i] = term


def mix_kernel(offsets, weight_ref, out_ref, mem_ref, w_ref, head_ref, away_ref, keep_ref):
    heads, rows, _ = weight_ref.shape
    head_dim = out_ref.shape[1] // heads
    for h in range(heads):
        part = slice(h * head_dim, (h + 1) * head_dim)
        out = out_ref[:, part] + dot(weight_ref[h], mem_ref[:, part])
        head_ref[:, part] = out.astype(BF16)
    blocks_out(offsets, head_ref[...], w_ref, away_ref, keep_ref)


def rest_kernel(offsets, head_ref, w_ref, away_ref, keep_ref):
    blocks_out(offsets, head_ref[...], w_ref, away_ref, keep_ref)


def block_shapes(offsets, rows, width):
    count = len(offsets)
    return (pltpu.VMEM((count, rows, width), BF16), pltpu.VMEM((count, rows, width), F32))


def mix(offsets, weights, out, mem_val, w_out, width):
    rows, cols = out.shape
    return call(
        functools.partial(mix_kernel, offsets),
        (pltpu.VMEM((rows, cols), BF16),) + block_shapes(offsets, rows, width),
        [vmem_spec()] * 4,
        [],
        4 * rows * cols * width * len(offsets),
        4 * cols * width * len(offsets),
        "mix",
    )(weights, out, mem_val, w_out)


def rest(offsets, head_out, w_out, width):
    rows, cols = head_out.shape
    return call(
        functools.partial(rest_kernel, offsets),
        block_shapes(offsets, rows, width),
        [vmem_spec()] * 2,
        [],
        4 * rows * cols * width * len(offsets),
        4 * cols * width * len(offsets),
        "rest",
    )(head_out, w_out)


def shards(tokens, w_qkv, w_pos, w_out, content_bias, position_bias, doc_ids):
    rows = tokens.shape[0]
    count = lax.axis_size("mp")
    chips = count // 2
    segments = lax.axis_size("seq")
    width = w_out.shape[1] // count

    def across(value, k):
        return lax.ppermute(value, "mp", [(i, (i + 2 * k) % count) for i in range(count)])

    def swap(value):
        return lax.ppermute(value, "mp", [(i, i ^ 1) for i in range(count)])

    def onward(value):
        return lax.ppermute(value, "seq", [(i, (i + 1) % segments) for i in range(segments)])

    mine = [tokens] + [across(tokens, k) for k in range(1, chips)]
    other = [swap(tokens)]
    docs = (doc_ids + 1).astype(F32).reshape(1, rows)
    rel, w_kv = load(w_pos, w_qkv, 2 * rows)
    for k in range(1, chips):
        mine[k], rel = lax.optimization_barrier((mine[k], rel))
        other.append(swap(mine[k]))
    last = chips - 1
    acc = None
    for k in range(last):
        acc = kv_step({(k, 0): mine[k], (k, 1): other[k]}, w_kv, acc)
    part = {(last, 0): mine[last], (last, 1): other[last]}
    own_key = kv_step(part, w_kv, acc, (1,), "keys", docs, content_bias.shape[0])
    mem_key = onward(own_key)
    own_val = kv_step(part, w_kv, acc, (2,), "values")
    mem_val = onward(own_val)
    own_val, rel = lax.optimization_barrier((own_val, rel))
    query_content, score, w_out = queries(
        [chunk for pair in zip(mine, other) for chunk in pair],
        w_qkv,
        w_out,
        content_bias,
        position_bias,
        own_key,
        rel,
        docs,
    )
    weights, out = weigh(query_content, score, mem_key, own_val, docs)
    first = [chips // 2]
    others = [k for k in range(chips) if k not in first]
    head_out, away, keep = mix(first, weights, out, mem_val, w_out, width)
    total = {first[0]: keep[0] + swap(away)[0].astype(F32)}
    away, keep = rest(others, head_out, w_out, width)
    away, total[first[0]] = lax.optimization_barrier((away, total[first[0]]))
    away = swap(away).astype(F32)
    for i, k in enumerate(others):
        total[k] = keep[i] + away[i]
    result = total[0]
    for k in first + others:
        if k > 0:
            result = result + across(total[k].astype(BF16), k).astype(F32)
    return result.astype(BF16)


def solution(mesh):
    in_specs = (
        P("seq", "mp"),
        P(None, None, "mp"),
        P(None, "mp"),
        P("mp", None),
        P("mp", None),
        P("mp", None),
        P("seq"),
    )
    out_specs = P("seq", "mp")
    return jax.shard_map(shards, mesh=mesh, in_specs=in_specs, out_specs=out_specs, check_vma=False)
```

```python
import functools

import jax
import jax.numpy as jnp
from jax import lax
from jax.experimental import pallas as pl
from jax.experimental.pallas import tpu as pltpu
from jax.sharding import PartitionSpec as P

BF16 = jnp.bfloat16
F32 = jnp.float32
VMEM_LIMIT = 24 * 1024 * 1024


def vmem_spec():
    return pl.BlockSpec(memory_space=pltpu.VMEM)


def hbm_spec():
    return pl.BlockSpec(memory_space=pl.ANY)


def in_hbm(value):
    return pltpu.with_memory_space_constraint(value, pltpu.HBM)


def call(kernel, out_shape, in_specs, scratch, flops, nbytes, name, transcendentals=0):
    outs = jax.tree.map(lambda _: vmem_spec(), out_shape)
    return pl.pallas_call(
        kernel,
        out_shape=out_shape,
        in_specs=in_specs,
        out_specs=outs,
        scratch_shapes=scratch,
        compiler_params=pltpu.CompilerParams(vmem_limit_bytes=VMEM_LIMIT),
        cost_estimate=pl.CostEstimate(
            flops=flops, bytes_accessed=nbytes, transcendentals=transcendentals
        ),
        name=name,
    )


def dot(a, b):
    return jnp.dot(a, b, preferred_element_type=F32)


def dot_nt(a, b):
    return lax.dot_general(a, b, (((1,), (1,)), ((), ())), preferred_element_type=F32)


def load_kernel(parts, w_pos, w_qkv, rel_ref, kv_ref, wbuf, table, sems):
    rows, cols = rel_ref.shape
    width = w_pos.shape[0]
    half = width // 2
    depth = width // parts

    def pos_copy(i):
        part = pl.ds(i * depth, depth)
        return pltpu.make_async_copy(w_pos.at[part], wbuf.at[part], sems.at[i])

    copies = [pos_copy(i) for i in range(parts)]
    for c in range(2):
        copies.append(pltpu.make_async_copy(w_qkv.at[c + 1], kv_ref.at[c], sems.at[parts + c]))
    for item in copies:
        item.start()
    fine = 16
    coarse = rows // fine
    index = lax.broadcasted_iota(jnp.int32, (1, half), 1).astype(F32) * 2.0
    freqs = 1.0 / 10000.0 ** (index / width)
    low = (fine - 1 - lax.broadcasted_iota(jnp.int32, (fine, half), 0)).astype(F32) * freqs
    high = (lax.broadcasted_iota(jnp.int32, (coarse, half), 0) * fine).astype(F32) * freqs
    sin_low, cos_low = jnp.sin(low), jnp.cos(low)
    sin_high, cos_high = jnp.sin(high), jnp.cos(high)
    for a in range(coarse):
        sh, ch = sin_high[a : a + 1], cos_high[a : a + 1]
        first = (coarse - 1 - a) * fine
        table[first : first + fine, :half] = (sh * cos_low + ch * sin_low).astype(BF16)
        table[first : first + fine, half:] = (ch * cos_low - sh * sin_low).astype(BF16)
    total = jnp.zeros((rows, cols), F32)
    for i in range(parts):
        copies[i].wait()
        total = total + dot(
            table[:, i * depth : (i + 1) * depth], wbuf[i * depth : (i + 1) * depth]
        )
    rel_ref[...] = total.astype(BF16)
    for item in copies[parts:]:
        item.wait()


def load(w_pos, w_qkv, rows):
    width, cols = w_pos.shape
    parts = 8
    return call(
        functools.partial(load_kernel, parts),
        (pltpu.VMEM((rows, cols), BF16), pltpu.VMEM((2, width, cols), BF16)),
        [hbm_spec()] * 2,
        [
            pltpu.VMEM((width, cols), BF16),
            pltpu.VMEM((rows, width), BF16),
            pltpu.SemaphoreType.DMA((parts + 2,)),
        ],
        rows * width,
        rows * width,
        "load",
    )(in_hbm(w_pos), in_hbm(w_qkv))


def here(back):
    me = lax.axis_index("mp")
    chips = lax.axis_size("mp") // 2
    return lax.rem(me, 2), lax.rem(me // 2 + chips - back, chips)


def row_block(core, place, i):
    return 2 * place + (core if i == 0 else 1 - core)


def kv_kernel(sources, kinds, first, last, *refs):
    refs = list(refs)
    x_refs = [refs.pop(0) for _ in sources]
    w_ref = refs.pop(0)
    acc_ref = None if first else refs.pop(0)
    doc_ref = refs.pop(0) if last == "keys" else None
    (out_ref,) = refs
    rows, depth = x_refs[0].shape
    for kind in kinds:
        total = None if first else acc_ref[kind - 1]
        for (back, i), x_ref in zip(sources, x_refs):
            core, place = here(back)
            start = pl.multiple_of(row_block(core, place, i) * depth, depth)
            term = dot(x_ref[...], w_ref[kind - 1, pl.ds(start, depth)])
            total = term if total is None else total + term
        if last == "keys":
            head_dim = out_ref.shape[1]
            for h in range(total.shape[1] // head_dim):
                part = total[:, h * head_dim : (h + 1) * head_dim]
                out_ref[h * rows : (h + 1) * rows] = part.astype(BF16)
            docs = jnp.broadcast_to(doc_ref[...], (16, rows)).astype(BF16)
            out_ref[out_ref.shape[0] - 16 :] = docs
        elif last == "values":
            out_ref[...] = total.astype(BF16)
        else:
            out_ref[kind - 1] = total


def kv_step(chunks, w_qkv, acc, kinds=(1, 2), last=None, docs=None, heads=None):
    sources = tuple(chunks)
    rows, depth = chunks[sources[0]].shape
    cols = w_qkv.shape[2]
    args = [chunks[source] for source in sources] + [w_qkv]
    args += ([] if acc is None else [acc]) + ([] if docs is None else [docs])
    out = pltpu.VMEM((2, rows, cols), F32)
    if last == "keys":
        assert rows == cols // heads
        out = pltpu.VMEM((heads * rows + 16, cols // heads), BF16)
    elif last == "values":
        out = pltpu.VMEM((rows, cols), BF16)
    return call(
        functools.partial(kv_kernel, sources, kinds, acc is None, last),
        out,
        [vmem_spec()] * len(args),
        [],
        16 * rows * depth * cols,
        0,
        "kv_step",
    )(*args)


def q_kernel(count, heads, *refs):
    x_refs = refs[:count]
    w_ref, w_out, cb_ref, pb_ref, key_ref, rel_ref, doc_ref = refs[count : count + 7]
    qc_ref, score_ref, w_out_ref, wbuf, sems = refs[count + 7 :]
    rows, depth = x_refs[0].shape
    head_dim = qc_ref.shape[1] // heads

    def copy(i):
        core, place = here(i // 2)
        start = pl.multiple_of(row_block(core, place, i % 2) * depth, depth)
        return pltpu.make_async_copy(w_ref.at[0, pl.ds(start, depth)], wbuf.at[i], sems.at[i])

    copies = [copy(i) for i in range(count)]
    copies.append(pltpu.make_async_copy(w_out, w_out_ref, sems.at[count]))
    for item in copies:
        item.start()
    total = None
    for i in range(count):
        copies[i].wait()
        term = dot(x_refs[i][...], wbuf[i])
        total = term if total is None else total + term
    query_content = (total + cb_ref[...]).astype(BF16)
    query_pos = (total + pb_ref[...]).astype(BF16)
    qc_ref[...] = query_content
    query = lax.broadcasted_iota(jnp.int32, (rows, rows), 0)
    key = lax.broadcasted_iota(jnp.int32, (rows, rows), 1)
    own_doc = jnp.broadcast_to(doc_ref[...], (rows, rows))
    allowed = (key <= query) & (own_doc == own_doc.T)
    scale = 1.0 / (float(head_dim) ** 0.5)
    for h in range(heads):
        part = slice(h * head_dim, (h + 1) * head_dim)
        pos = pltpu.roll(
            dot_nt(query_pos[:, part], rel_ref[:, part]), rows + 1, 1, stride=1, stride_axis=0
        )
        content = dot_nt(query_content[:, part], key_ref[h * rows : (h + 1) * rows])
        score_ref[h, :, :rows] = pos[:, :rows]
        score_ref[h, :, rows:] = jnp.where(allowed, (content + pos[:, rows:]) * scale, -1e30)
    copies[count].wait()


def queries(chunks, w_qkv, w_out, content_bias, position_bias, own_key, rel, docs):
    count = len(chunks)
    rows, depth = chunks[0].shape
    cols = w_qkv.shape[2]
    heads = content_bias.shape[0]
    return call(
        functools.partial(q_kernel, count, heads),
        (
            pltpu.VMEM((rows, cols), BF16),
            pltpu.VMEM((heads, rows, 2 * rows), F32),
            pltpu.VMEM(w_out.shape, BF16),
        ),
        [vmem_spec()] * count + [hbm_spec()] * 2 + [vmem_spec()] * 5,
        [pltpu.VMEM((count, depth, cols), BF16), pltpu.SemaphoreType.DMA((count + 1,))],
        2 * count * rows * depth * cols,
        2 * count * depth * cols,
        "queries",
    )(
        *chunks,
        in_hbm(w_qkv),
        in_hbm(w_out),
        content_bias.reshape(1, cols),
        position_bias.reshape(1, cols),
        own_key,
        rel,
        docs,
    )


def weigh_kernel(qc_ref, score_ref, mem_ref, val_ref, doc_ref, weight_ref, out_ref):
    heads, rows, _ = score_ref.shape
    head_dim = qc_ref.shape[1] // heads
    exists = jnp.minimum(lax.axis_index("seq"), 1).astype(F32)
    mem_doc = mem_ref[heads * rows : heads * rows + 1].astype(F32) * exists
    mem_doc = jnp.broadcast_to(mem_doc, (rows, rows))
    allowed = mem_doc == jnp.broadcast_to(doc_ref[...], (rows, rows)).T
    scale = 1.0 / (float(head_dim) ** 0.5)
    for h in range(heads):
        part = slice(h * head_dim, (h + 1) * head_dim)
        content = dot_nt(qc_ref[:, part], mem_ref[h * rows : (h + 1) * rows])
        mem = jnp.where(allowed, (content + score_ref[h, :, :rows]) * scale, -1e30)
        own = score_ref[h, :, rows:]
        top = jnp.maximum(
            jnp.max(mem, axis=1, keepdims=True), jnp.max(own, axis=1, keepdims=True)
        )
        mem = jnp.where(mem > -1e29, jnp.exp(mem - top), 0.0)
        own = jnp.where(own > -1e29, jnp.exp(own - top), 0.0)
        total = jnp.sum(mem, axis=1, keepdims=True) + jnp.sum(own, axis=1, keepdims=True)
        weight_ref[h] = (mem / total).astype(BF16)
        out_ref[:, part] = dot((own / total).astype(BF16), val_ref[:, part])


def weigh(query_content, score, mem_key, own_val, docs):
    rows, cols = query_content.shape
    heads = score.shape[0]
    return call(
        weigh_kernel,
        (pltpu.VMEM((heads, rows, rows), BF16), pltpu.VMEM((rows, cols), F32)),
        [vmem_spec()] * 5,
        [],
        8 * rows * rows * cols,
        8 * rows * cols,
        "weigh",
    )(query_content, score, mem_key, own_val, docs)


def blocks_out(away, offsets, head_out, w_ref, out_ref):
    width = out_ref.shape[2]
    core, chip = here(0)
    chips = lax.axis_size("mp") // 2
    for i, k in enumerate(offsets):
        block = 2 * lax.rem(chip + k, chips) + (1 - core if away else core)
        start = pl.multiple_of(block * width, width)
        out_ref[i] = dot(head_out, w_ref[:, pl.ds(start, width)]).astype(out_ref.dtype)


def mix_kernel(first, weight_ref, out_ref, mem_ref, w_ref, head_ref, away_ref):
    heads, rows, _ = weight_ref.shape
    head_dim = out_ref.shape[1] // heads
    for h in range(heads):
        part = slice(h * head_dim, (h + 1) * head_dim)
        out = out_ref[:, part] + dot(weight_ref[h], mem_ref[:, part])
        head_ref[:, part] = out.astype(BF16)
    blocks_out(True, [first], head_ref[...], w_ref, away_ref)


def mix(first, weights, out, mem_val, w_out, width):
    rows, cols = out.shape
    return call(
        functools.partial(mix_kernel, first),
        (pltpu.VMEM((rows, cols), BF16), pltpu.VMEM((1, rows, width), BF16)),
        [vmem_spec()] * 4,
        [],
        2 * rows * cols * width,
        2 * cols * width,
        "mix",
    )(weights, out, mem_val, w_out)


def rest_kernel(others, kept, head_ref, w_ref, away_ref, keep_ref):
    blocks_out(True, others, head_ref[...], w_ref, away_ref)
    blocks_out(False, kept, head_ref[...], w_ref, keep_ref)


def rest(others, kept, head_out, w_out, width):
    rows, cols = head_out.shape
    return call(
        functools.partial(rest_kernel, others, kept),
        (
            pltpu.VMEM((len(others), rows, width), BF16),
            pltpu.VMEM((len(kept), rows, width), F32),
        ),
        [vmem_spec()] * 2,
        [],
        4 * rows * cols * width * len(kept),
        4 * cols * width * len(kept),
        "rest",
    )(head_out, w_out)


def shards(tokens, w_qkv, w_pos, w_out, content_bias, position_bias, doc_ids):
    rows = tokens.shape[0]
    count = lax.axis_size("mp")
    chips = count // 2
    segments = lax.axis_size("seq")
    width = w_out.shape[1] // count

    def across(value, k):
        return lax.ppermute(value, "mp", [(i, (i + 2 * k) % count) for i in range(count)])

    def swap(value):
        return lax.ppermute(value, "mp", [(i, i ^ 1) for i in range(count)])

    def onward(value):
        return lax.ppermute(value, "seq", [(i, (i + 1) % segments) for i in range(segments)])

    mine = [tokens] + [across(tokens, k) for k in range(1, chips)]
    other = [swap(tokens)]
    docs = (doc_ids + 1).astype(F32).reshape(1, rows)
    rel, w_kv = load(w_pos, w_qkv, 2 * rows)
    for k in range(1, chips):
        mine[k], rel = lax.optimization_barrier((mine[k], rel))
        other.append(swap(mine[k]))
    last = chips - 1
    acc = None
    for k in range(last):
        acc = kv_step({(k, 0): mine[k], (k, 1): other[k]}, w_kv, acc)
    part = {(last, 0): mine[last], (last, 1): other[last]}
    own_key = kv_step(part, w_kv, acc, (1,), "keys", docs, content_bias.shape[0])
    mem_key = onward(own_key)
    own_val = kv_step(part, w_kv, acc, (2,), "values")
    mem_val = onward(own_val)
    own_val, rel = lax.optimization_barrier((own_val, rel))
    query_content, score, w_out = queries(
        [chunk for pair in zip(mine, other) for chunk in pair],
        w_qkv,
        w_out,
        content_bias,
        position_bias,
        own_key,
        rel,
        docs,
    )
    weights, out = weigh(query_content, score, mem_key, own_val, docs)
    first = chips // 2
    others = [k for k in range(chips) if k != first]
    head_out, away = mix(first, weights, out, mem_val, w_out, width)
    swapped = swap(away)
    away, keep = rest(others, [first] + others, head_out, w_out, width)
    total = {first: keep[0] + swapped[0].astype(F32)}
    away, total[first] = lax.optimization_barrier((away, total[first]))
    away = swap(away)
    for i, k in enumerate(others):
        total[k] = keep[i + 1] + away[i].astype(F32)
    result = total[0]
    for k in [first] + others:
        if k > 0:
            result = result + across(total[k].astype(BF16), k).astype(F32)
    return result.astype(BF16)


def solution(mesh):
    in_specs = (
        P("seq", "mp"),
        P(None, None, "mp"),
        P(None, "mp"),
        P("mp", None),
        P("mp", None),
        P("mp", None),
        P("seq"),
    )
    out_specs = P("seq", "mp")
    return jax.shard_map(shards, mesh=mesh, in_specs=in_specs, out_specs=out_specs, check_vma=False)
```

```python
import functools

import jax
import jax.numpy as jnp
from jax import lax
from jax.experimental import pallas as pl
from jax.experimental.pallas import tpu as pltpu
from jax.sharding import PartitionSpec as P

BF16 = jnp.bfloat16
F32 = jnp.float32
VMEM_LIMIT = 24 * 1024 * 1024


def vmem_spec():
    return pl.BlockSpec(memory_space=pltpu.VMEM)


def hbm_spec():
    return pl.BlockSpec(memory_space=pl.ANY)


def in_hbm(value):
    return pltpu.with_memory_space_constraint(value, pltpu.HBM)


def call(kernel, out_shape, in_specs, scratch, flops, nbytes, name, transcendentals=0):
    outs = jax.tree.map(lambda _: vmem_spec(), out_shape)
    return pl.pallas_call(
        kernel,
        out_shape=out_shape,
        in_specs=in_specs,
        out_specs=outs,
        scratch_shapes=scratch,
        compiler_params=pltpu.CompilerParams(vmem_limit_bytes=VMEM_LIMIT),
        cost_estimate=pl.CostEstimate(
            flops=flops, bytes_accessed=nbytes, transcendentals=transcendentals
        ),
        name=name,
    )


def dot(a, b):
    return jnp.dot(a, b, preferred_element_type=F32)


def dot_nt(a, b):
    return lax.dot_general(a, b, (((1,), (1,)), ((), ())), preferred_element_type=F32)


def load_kernel(parts, w_pos, w_qkv, rel_ref, kv_ref, wbuf, table, sems):
    rows, cols = rel_ref.shape
    width = w_pos.shape[0]
    half = width // 2
    depth = width // parts

    def pos_copy(i):
        part = pl.ds(i * depth, depth)
        return pltpu.make_async_copy(w_pos.at[part], wbuf.at[part], sems.at[i])

    copies = [pos_copy(i) for i in range(parts)]
    for c in range(2):
        copies.append(pltpu.make_async_copy(w_qkv.at[c + 1], kv_ref.at[c], sems.at[parts + c]))
    for item in copies:
        item.start()
    fine = 16
    coarse = rows // fine
    index = lax.broadcasted_iota(jnp.int32, (1, half), 1).astype(F32) * 2.0
    freqs = 1.0 / 10000.0 ** (index / width)
    low = (fine - 1 - lax.broadcasted_iota(jnp.int32, (fine, half), 0)).astype(F32) * freqs
    high = (lax.broadcasted_iota(jnp.int32, (coarse, half), 0) * fine).astype(F32) * freqs
    sin_low, cos_low = jnp.sin(low), jnp.cos(low)
    sin_high, cos_high = jnp.sin(high), jnp.cos(high)
    for a in range(coarse):
        sh, ch = sin_high[a : a + 1], cos_high[a : a + 1]
        first = (coarse - 1 - a) * fine
        table[first : first + fine, :half] = (sh * cos_low + ch * sin_low).astype(BF16)
        table[first : first + fine, half:] = (ch * cos_low - sh * sin_low).astype(BF16)
    total = jnp.zeros((rows, cols), F32)
    for i in range(parts):
        copies[i].wait()
        total = total + dot(
            table[:, i * depth : (i + 1) * depth], wbuf[i * depth : (i + 1) * depth]
        )
    rel_ref[...] = total.astype(BF16)
    for item in copies[parts:]:
        item.wait()


def load(w_pos, w_qkv, rows):
    width, cols = w_pos.shape
    parts = 8
    return call(
        functools.partial(load_kernel, parts),
        (pltpu.VMEM((rows, cols), BF16), pltpu.VMEM((2, width, cols), BF16)),
        [hbm_spec()] * 2,
        [
            pltpu.VMEM((width, cols), BF16),
            pltpu.VMEM((rows, width), BF16),
            pltpu.SemaphoreType.DMA((parts + 2,)),
        ],
        rows * width,
        rows * width,
        "load",
    )(in_hbm(w_pos), in_hbm(w_qkv))


def here(back):
    me = lax.axis_index("mp")
    chips = lax.axis_size("mp") // 2
    return lax.rem(me, 2), lax.rem(me // 2 + chips - back, chips)


def row_block(core, place, i):
    return 2 * place + (core if i == 0 else 1 - core)


def kv_kernel(sources, kinds, first, last, *refs):
    refs = list(refs)
    x_refs = [refs.pop(0) for _ in sources]
    w_ref = refs.pop(0)
    acc_ref = None if first else refs.pop(0)
    doc_ref = refs.pop(0) if last == "keys" else None
    (out_ref,) = refs
    rows, depth = x_refs[0].shape
    for kind in kinds:
        total = None if first else acc_ref[kind - 1]
        for (back, i), x_ref in zip(sources, x_refs):
            core, place = here(back)
            start = pl.multiple_of(row_block(core, place, i) * depth, depth)
            term = dot(x_ref[...], w_ref[kind - 1, pl.ds(start, depth)])
            total = term if total is None else total + term
        if last == "keys":
            head_dim = out_ref.shape[1]
            for h in range(total.shape[1] // head_dim):
                part = total[:, h * head_dim : (h + 1) * head_dim]
                out_ref[h * rows : (h + 1) * rows] = part.astype(BF16)
            docs = jnp.broadcast_to(doc_ref[...], (16, rows)).astype(BF16)
            out_ref[out_ref.shape[0] - 16 :] = docs
        elif last == "values":
            out_ref[...] = total.astype(BF16)
        else:
            out_ref[kind - 1] = total


def kv_step(chunks, w_qkv, acc, kinds=(1, 2), last=None, docs=None, heads=None):
    sources = tuple(chunks)
    rows, depth = chunks[sources[0]].shape
    cols = w_qkv.shape[2]
    args = [chunks[source] for source in sources] + [w_qkv]
    args += ([] if acc is None else [acc]) + ([] if docs is None else [docs])
    out = pltpu.VMEM((2, rows, cols), F32)
    if last == "keys":
        assert rows == cols // heads
        out = pltpu.VMEM((heads * rows + 16, cols // heads), BF16)
    elif last == "values":
        out = pltpu.VMEM((rows, cols), BF16)
    return call(
        functools.partial(kv_kernel, sources, kinds, acc is None, last),
        out,
        [vmem_spec()] * len(args),
        [],
        16 * rows * depth * cols,
        0,
        "kv_step",
    )(*args)


def q_kernel(count, heads, *refs):
    x_refs = refs[:count]
    w_ref, w_out, cb_ref, pb_ref, key_ref, rel_ref, doc_ref = refs[count : count + 7]
    qc_ref, score_ref, w_out_ref, wbuf, sems = refs[count + 7 :]
    rows, depth = x_refs[0].shape
    head_dim = qc_ref.shape[1] // heads

    def copy(i):
        core, place = here(i // 2)
        start = pl.multiple_of(row_block(core, place, i % 2) * depth, depth)
        return pltpu.make_async_copy(w_ref.at[0, pl.ds(start, depth)], wbuf.at[i], sems.at[i])

    copies = [copy(i) for i in range(count)]
    copies.append(pltpu.make_async_copy(w_out, w_out_ref, sems.at[count]))
    for item in copies:
        item.start()
    total = None
    for i in range(count):
        copies[i].wait()
        term = dot(x_refs[i][...], wbuf[i])
        total = term if total is None else total + term
    query_content = (total + cb_ref[...]).astype(BF16)
    query_pos = (total + pb_ref[...]).astype(BF16)
    qc_ref[...] = query_content
    query = lax.broadcasted_iota(jnp.int32, (rows, rows), 0)
    key = lax.broadcasted_iota(jnp.int32, (rows, rows), 1)
    own_doc = jnp.broadcast_to(doc_ref[...], (rows, rows))
    allowed = (key <= query) & (own_doc == own_doc.T)
    scale = 1.0 / (float(head_dim) ** 0.5)
    for h in range(heads):
        part = slice(h * head_dim, (h + 1) * head_dim)
        pos = pltpu.roll(
            dot_nt(query_pos[:, part], rel_ref[:, part]), rows + 1, 1, stride=1, stride_axis=0
        )
        content = dot_nt(query_content[:, part], key_ref[h * rows : (h + 1) * rows])
        score_ref[h, :, :rows] = pos[:, :rows]
        score_ref[h, :, rows:] = jnp.where(allowed, (content + pos[:, rows:]) * scale, -1e30)
    copies[count].wait()


def queries(chunks, w_qkv, w_out, content_bias, position_bias, own_key, rel, docs):
    count = len(chunks)
    rows, depth = chunks[0].shape
    cols = w_qkv.shape[2]
    heads = content_bias.shape[0]
    return call(
        functools.partial(q_kernel, count, heads),
        (
            pltpu.VMEM((rows, cols), BF16),
            pltpu.VMEM((heads, rows, 2 * rows), F32),
            pltpu.VMEM(w_out.shape, BF16),
        ),
        [vmem_spec()] * count + [hbm_spec()] * 2 + [vmem_spec()] * 5,
        [pltpu.VMEM((count, depth, cols), BF16), pltpu.SemaphoreType.DMA((count + 1,))],
        2 * count * rows * depth * cols,
        2 * count * depth * cols,
        "queries",
    )(
        *chunks,
        in_hbm(w_qkv),
        in_hbm(w_out),
        content_bias.reshape(1, cols),
        position_bias.reshape(1, cols),
        own_key,
        rel,
        docs,
    )


def weigh_kernel(qc_ref, score_ref, mem_ref, val_ref, doc_ref, weight_ref, out_ref):
    heads, rows, _ = score_ref.shape
    head_dim = qc_ref.shape[1] // heads
    exists = jnp.minimum(lax.axis_index("seq"), 1).astype(F32)
    mem_doc = mem_ref[heads * rows : heads * rows + 16].astype(F32)[:1] * exists
    mem_doc = jnp.broadcast_to(mem_doc, (rows, rows))
    allowed = mem_doc == jnp.broadcast_to(doc_ref[...], (rows, rows)).T
    scale = 1.0 / (float(head_dim) ** 0.5)
    for h in range(heads):
        part = slice(h * head_dim, (h + 1) * head_dim)
        content = dot_nt(qc_ref[:, part], mem_ref[h * rows : (h + 1) * rows])
        mem = jnp.where(allowed, (content + score_ref[h, :, :rows]) * scale, -1e30)
        own = score_ref[h, :, rows:]
        top = jnp.maximum(
            jnp.max(mem, axis=1, keepdims=True), jnp.max(own, axis=1, keepdims=True)
        )
        mem = jnp.where(mem > -1e29, jnp.exp(mem - top), 0.0)
        own = jnp.where(own > -1e29, jnp.exp(own - top), 0.0)
        total = jnp.sum(mem, axis=1, keepdims=True) + jnp.sum(own, axis=1, keepdims=True)
        weight_ref[h] = (mem / total).astype(BF16)
        out_ref[:, part] = dot((own / total).astype(BF16), val_ref[:, part])


def weigh(query_content, score, mem_key, own_val, docs):
    rows, cols = query_content.shape
    heads = score.shape[0]
    return call(
        weigh_kernel,
        (pltpu.VMEM((heads, rows, rows), BF16), pltpu.VMEM((rows, cols), F32)),
        [vmem_spec()] * 5,
        [],
        8 * rows * rows * cols,
        8 * rows * cols,
        "weigh",
    )(query_content, score, mem_key, own_val, docs)


def blocks_out(away, offsets, head_out, w_ref, out_ref):
    width = out_ref.shape[2]
    core, chip = here(0)
    chips = lax.axis_size("mp") // 2
    for i, k in enumerate(offsets):
        block = 2 * lax.rem(chip + k, chips) + (1 - core if away else core)
        start = pl.multiple_of(block * width, width)
        out_ref[i] = dot(head_out, w_ref[:, pl.ds(start, width)]).astype(out_ref.dtype)


def mix_kernel(first, weight_ref, out_ref, mem_ref, w_ref, head_ref, away_ref):
    heads, rows, _ = weight_ref.shape
    head_dim = out_ref.shape[1] // heads
    for h in range(heads):
        part = slice(h * head_dim, (h + 1) * head_dim)
        out = out_ref[:, part] + dot(weight_ref[h], mem_ref[:, part])
        head_ref[:, part] = out.astype(BF16)
    blocks_out(True, [first], head_ref[...], w_ref, away_ref)


def mix(first, weights, out, mem_val, w_out, width):
    rows, cols = out.shape
    return call(
        functools.partial(mix_kernel, first),
        (pltpu.VMEM((rows, cols), BF16), pltpu.VMEM((1, rows, width), BF16)),
        [vmem_spec()] * 4,
        [],
        2 * rows * cols * width,
        2 * cols * width,
        "mix",
    )(weights, out, mem_val, w_out)


def rest_kernel(others, kept, head_ref, w_ref, away_ref, keep_ref):
    blocks_out(True, others, head_ref[...], w_ref, away_ref)
    blocks_out(False, kept, head_ref[...], w_ref, keep_ref)


def rest(others, kept, head_out, w_out, width):
    rows, cols = head_out.shape
    return call(
        functools.partial(rest_kernel, others, kept),
        (
            pltpu.VMEM((len(others), rows, width), BF16),
            pltpu.VMEM((len(kept), rows, width), F32),
        ),
        [vmem_spec()] * 2,
        [],
        4 * rows * cols * width * len(kept),
        4 * cols * width * len(kept),
        "rest",
    )(head_out, w_out)


def shards(tokens, w_qkv, w_pos, w_out, content_bias, position_bias, doc_ids):
    rows = tokens.shape[0]
    count = lax.axis_size("mp")
    chips = count // 2
    segments = lax.axis_size("seq")
    width = w_out.shape[1] // count

    def across(value, k):
        return lax.ppermute(value, "mp", [(i, (i + 2 * k) % count) for i in range(count)])

    def swap(value):
        return lax.ppermute(value, "mp", [(i, i ^ 1) for i in range(count)])

    def onward(value):
        return lax.ppermute(value, "seq", [(i, (i + 1) % segments) for i in range(segments)])

    mine = [tokens] + [across(tokens, k) for k in range(1, chips)]
    other = [swap(tokens)]
    docs = (doc_ids + 1).astype(F32).reshape(1, rows)
    rel, w_kv = load(w_pos, w_qkv, 2 * rows)
    for k in range(1, chips):
        mine[k], rel = lax.optimization_barrier((mine[k], rel))
        other.append(swap(mine[k]))
    last = chips - 1
    acc = None
    for k in range(last):
        acc = kv_step({(k, 0): mine[k], (k, 1): other[k]}, w_kv, acc)
    part = {(last, 0): mine[last], (last, 1): other[last]}
    own_key = kv_step(part, w_kv, acc, (1,), "keys", docs, content_bias.shape[0])
    mem_key = onward(own_key)
    own_val = kv_step(part, w_kv, acc, (2,), "values")
    mem_val = onward(own_val)
    own_val, rel = lax.optimization_barrier((own_val, rel))
    query_content, score, w_out = queries(
        [chunk for pair in zip(mine, other) for chunk in pair],
        w_qkv,
        w_out,
        content_bias,
        position_bias,
        own_key,
        rel,
        docs,
    )
    weights, out = weigh(query_content, score, mem_key, own_val, docs)
    first = chips // 2
    others = [k for k in range(chips) if k != first]
    head_out, away = mix(first, weights, out, mem_val, w_out, width)
    swapped = swap(away)
    away, keep = rest(others, [first] + others, head_out, w_out, width)
    total = {first: keep[0] + swapped[0].astype(F32)}
    away, total[first] = lax.optimization_barrier((away, total[first]))
    away = swap(away)
    for i, k in enumerate(others):
        total[k] = keep[i + 1] + away[i].astype(F32)
    result = total[0]
    for k in [first] + others:
        if k > 0:
            result = result + across(total[k].astype(BF16), k).astype(F32)
    return result.astype(BF16)


def solution(mesh):
    in_specs = (
        P("seq", "mp"),
        P(None, None, "mp"),
        P(None, "mp"),
        P("mp", None),
        P("mp", None),
        P("mp", None),
        P("seq"),
    )
    out_specs = P("seq", "mp")
    return jax.shard_map(shards, mesh=mesh, in_specs=in_specs, out_specs=out_specs, check_vma=False)
```

```python
import functools

import jax
import jax.numpy as jnp
from jax import lax
from jax.experimental import pallas as pl
from jax.experimental.pallas import tpu as pltpu
from jax.sharding import PartitionSpec as P

BF16 = jnp.bfloat16
F32 = jnp.float32
VMEM_LIMIT = 16 * 1024 * 1024


def vmem_spec():
    return pl.BlockSpec(memory_space=pltpu.VMEM)


def hbm_spec():
    return pl.BlockSpec(memory_space=pl.ANY)


def in_hbm(value):
    return pltpu.with_memory_space_constraint(value, pltpu.HBM)


def call(kernel, out_shape, in_specs, scratch, flops, nbytes, name, transcendentals=0):
    outs = jax.tree.map(lambda _: vmem_spec(), out_shape)
    return pl.pallas_call(
        kernel,
        out_shape=out_shape,
        in_specs=in_specs,
        out_specs=outs,
        scratch_shapes=scratch,
        compiler_params=pltpu.CompilerParams(vmem_limit_bytes=VMEM_LIMIT),
        cost_estimate=pl.CostEstimate(
            flops=flops, bytes_accessed=nbytes, transcendentals=transcendentals
        ),
        name=name,
    )


def dot(a, b):
    return jnp.dot(a, b, preferred_element_type=F32)


def dot_nt(a, b):
    return lax.dot_general(a, b, (((1,), (1,)), ((), ())), preferred_element_type=F32)


def load_kernel(parts, w_pos, w_qkv, rel_ref, kv_ref, wbuf, table, sems):
    rows, cols = rel_ref.shape
    width = w_pos.shape[0]
    half = width // 2
    depth = width // parts

    def pos_copy(i):
        part = pl.ds(i * depth, depth)
        return pltpu.make_async_copy(w_pos.at[part], wbuf.at[part], sems.at[i])

    copies = [pos_copy(i) for i in range(parts)]
    for c in range(2):
        copies.append(pltpu.make_async_copy(w_qkv.at[c + 1], kv_ref.at[c], sems.at[parts + c]))
    for item in copies:
        item.start()
    fine = 16
    coarse = rows // fine
    index = lax.broadcasted_iota(jnp.int32, (1, half), 1).astype(F32) * 2.0
    freqs = 1.0 / 10000.0 ** (index / width)
    low = (fine - 1 - lax.broadcasted_iota(jnp.int32, (fine, half), 0)).astype(F32) * freqs
    high = (lax.broadcasted_iota(jnp.int32, (coarse, half), 0) * fine).astype(F32) * freqs
    sin_low, cos_low = jnp.sin(low), jnp.cos(low)
    sin_high, cos_high = jnp.sin(high), jnp.cos(high)
    for a in range(coarse):
        sh, ch = sin_high[a : a + 1], cos_high[a : a + 1]
        first = (coarse - 1 - a) * fine
        table[first : first + fine, :half] = (sh * cos_low + ch * sin_low).astype(BF16)
        table[first : first + fine, half:] = (ch * cos_low - sh * sin_low).astype(BF16)
    total = jnp.zeros((rows, cols), F32)
    for i in range(parts):
        copies[i].wait()
        total = total + dot(
            table[:, i * depth : (i + 1) * depth], wbuf[i * depth : (i + 1) * depth]
        )
    rel_ref[...] = total.astype(BF16)
    for item in copies[parts:]:
        item.wait()


def load(w_pos, w_qkv, rows):
    width, cols = w_pos.shape
    parts = 8
    return call(
        functools.partial(load_kernel, parts),
        (pltpu.VMEM((rows, cols), BF16), pltpu.VMEM((2, width, cols), BF16)),
        [hbm_spec()] * 2,
        [
            pltpu.VMEM((width, cols), BF16),
            pltpu.VMEM((rows, width), BF16),
            pltpu.SemaphoreType.DMA((parts + 2,)),
        ],
        rows * width,
        rows * width,
        "load",
    )(in_hbm(w_pos), in_hbm(w_qkv))


def here(back):
    me = lax.axis_index("mp")
    chips = lax.axis_size("mp") // 2
    return lax.rem(me, 2), lax.rem(me // 2 + chips - back, chips)


def row_block(core, place, i):
    return 2 * place + (core if i == 0 else 1 - core)


def kv_kernel(sources, kinds, first, last, *refs):
    refs = list(refs)
    x_refs = [refs.pop(0) for _ in sources]
    w_ref = refs.pop(0)
    acc_ref = None if first else refs.pop(0)
    doc_ref = refs.pop(0) if last == "keys" else None
    (out_ref,) = refs
    rows, depth = x_refs[0].shape
    for kind in kinds:
        total = None if first else acc_ref[kind - 1]
        for (back, i), x_ref in zip(sources, x_refs):
            core, place = here(back)
            start = pl.multiple_of(row_block(core, place, i) * depth, depth)
            term = dot(x_ref[...], w_ref[kind - 1, pl.ds(start, depth)])
            total = term if total is None else total + term
        if last == "keys":
            head_dim = out_ref.shape[1]
            for h in range(total.shape[1] // head_dim):
                part = total[:, h * head_dim : (h + 1) * head_dim]
                out_ref[h * rows : (h + 1) * rows] = part.astype(BF16)
            docs = jnp.broadcast_to(doc_ref[...], (16, rows)).astype(BF16)
            out_ref[out_ref.shape[0] - 16 :] = docs
        elif last == "values":
            out_ref[...] = total.astype(BF16)
        else:
            out_ref[kind - 1] = total


def kv_step(chunks, w_qkv, acc, kinds=(1, 2), last=None, docs=None, heads=None):
    sources = tuple(chunks)
    rows, depth = chunks[sources[0]].shape
    cols = w_qkv.shape[2]
    args = [chunks[source] for source in sources] + [w_qkv]
    args += ([] if acc is None else [acc]) + ([] if docs is None else [docs])
    out = pltpu.VMEM((2, rows, cols), F32)
    if last == "keys":
        assert rows == cols // heads
        out = pltpu.VMEM((heads * rows + 16, cols // heads), BF16)
    elif last == "values":
        out = pltpu.VMEM((rows, cols), BF16)
    return call(
        functools.partial(kv_kernel, sources, kinds, acc is None, last),
        out,
        [vmem_spec()] * len(args),
        [],
        16 * rows * depth * cols,
        0,
        "kv_step",
    )(*args)


def q_kernel(count, heads, *refs):
    x_refs = refs[:count]
    w_ref, w_out, cb_ref, pb_ref, key_ref, rel_ref, doc_ref = refs[count : count + 7]
    qc_ref, score_ref, w_out_ref, wbuf, sems = refs[count + 7 :]
    rows, depth = x_refs[0].shape
    head_dim = qc_ref.shape[1] // heads

    def copy(i):
        core, place = here(i // 2)
        start = pl.multiple_of(row_block(core, place, i % 2) * depth, depth)
        return pltpu.make_async_copy(w_ref.at[0, pl.ds(start, depth)], wbuf.at[i], sems.at[i])

    copies = [copy(i) for i in range(count)]
    copies.append(pltpu.make_async_copy(w_out, w_out_ref, sems.at[count]))
    for item in copies:
        item.start()
    total = None
    for i in range(count):
        copies[i].wait()
        term = dot(x_refs[i][...], wbuf[i])
        total = term if total is None else total + term
    query_content = (total + cb_ref[...]).astype(BF16)
    query_pos = (total + pb_ref[...]).astype(BF16)
    qc_ref[...] = query_content
    query = lax.broadcasted_iota(jnp.int32, (rows, rows), 0)
    key = lax.broadcasted_iota(jnp.int32, (rows, rows), 1)
    own_doc = jnp.broadcast_to(doc_ref[...], (rows, rows))
    allowed = (key <= query) & (own_doc == own_doc.T)
    scale = 1.0 / (float(head_dim) ** 0.5)
    for h in range(heads):
        part = slice(h * head_dim, (h + 1) * head_dim)
        pos = pltpu.roll(
            dot_nt(query_pos[:, part], rel_ref[:, part]), rows + 1, 1, stride=1, stride_axis=0
        )
        content = dot_nt(query_content[:, part], key_ref[h * rows : (h + 1) * rows])
        score_ref[h, :, :rows] = pos[:, :rows]
        score_ref[h, :, rows:] = jnp.where(allowed, (content + pos[:, rows:]) * scale, -1e30)
    copies[count].wait()


def queries(chunks, w_qkv, w_out, content_bias, position_bias, own_key, rel, docs):
    count = len(chunks)
    rows, depth = chunks[0].shape
    cols = w_qkv.shape[2]
    heads = content_bias.shape[0]
    return call(
        functools.partial(q_kernel, count, heads),
        (
            pltpu.VMEM((rows, cols), BF16),
            pltpu.VMEM((heads, rows, 2 * rows), F32),
            pltpu.VMEM(w_out.shape, BF16),
        ),
        [vmem_spec()] * count + [hbm_spec()] * 2 + [vmem_spec()] * 5,
        [pltpu.VMEM((count, depth, cols), BF16), pltpu.SemaphoreType.DMA((count + 1,))],
        2 * count * rows * depth * cols,
        2 * count * depth * cols,
        "queries",
    )(
        *chunks,
        in_hbm(w_qkv),
        in_hbm(w_out),
        content_bias.reshape(1, cols),
        position_bias.reshape(1, cols),
        own_key,
        rel,
        docs,
    )


def weigh_kernel(qc_ref, score_ref, mem_ref, val_ref, doc_ref, weight_ref, out_ref):
    heads, rows, _ = score_ref.shape
    head_dim = qc_ref.shape[1] // heads
    exists = jnp.minimum(lax.axis_index("seq"), 1).astype(F32)
    mem_doc = mem_ref[heads * rows : heads * rows + 16].astype(F32)[:1] * exists
    mem_doc = jnp.broadcast_to(mem_doc, (rows, rows))
    allowed = mem_doc == jnp.broadcast_to(doc_ref[...], (rows, rows)).T
    scale = 1.0 / (float(head_dim) ** 0.5)
    for h in range(heads):
        part = slice(h * head_dim, (h + 1) * head_dim)
        content = dot_nt(qc_ref[:, part], mem_ref[h * rows : (h + 1) * rows])
        mem = jnp.where(allowed, (content + score_ref[h, :, :rows]) * scale, -1e30)
        own = score_ref[h, :, rows:]
        top = jnp.maximum(
            jnp.max(mem, axis=1, keepdims=True), jnp.max(own, axis=1, keepdims=True)
        )
        mem = jnp.where(mem > -1e29, jnp.exp(mem - top), 0.0)
        own = jnp.where(own > -1e29, jnp.exp(own - top), 0.0)
        total = jnp.sum(mem, axis=1, keepdims=True) + jnp.sum(own, axis=1, keepdims=True)
        weight_ref[h] = (mem / total).astype(BF16)
        out_ref[:, part] = dot((own / total).astype(BF16), val_ref[:, part])


def weigh(query_content, score, mem_key, own_val, docs):
    rows, cols = query_content.shape
    heads = score.shape[0]
    return call(
        weigh_kernel,
        (pltpu.VMEM((heads, rows, rows), BF16), pltpu.VMEM((rows, cols), F32)),
        [vmem_spec()] * 5,
        [],
        8 * rows * rows * cols,
        8 * rows * cols,
        "weigh",
    )(query_content, score, mem_key, own_val, docs)


def blocks_out(away, offsets, head_out, w_ref, out_ref):
    width = out_ref.shape[2]
    core, chip = here(0)
    chips = lax.axis_size("mp") // 2
    for i, k in enumerate(offsets):
        block = 2 * lax.rem(chip + k, chips) + (1 - core if away else core)
        start = pl.multiple_of(block * width, width)
        out_ref[i] = dot(head_out, w_ref[:, pl.ds(start, width)]).astype(out_ref.dtype)


def mix_kernel(first, weight_ref, out_ref, mem_ref, w_ref, head_ref, away_ref):
    heads, rows, _ = weight_ref.shape
    head_dim = out_ref.shape[1] // heads
    for h in range(heads):
        part = slice(h * head_dim, (h + 1) * head_dim)
        out = out_ref[:, part] + dot(weight_ref[h], mem_ref[:, part])
        head_ref[:, part] = out.astype(BF16)
    blocks_out(True, [first], head_ref[...], w_ref, away_ref)


def mix(first, weights, out, mem_val, w_out, width):
    rows, cols = out.shape
    return call(
        functools.partial(mix_kernel, first),
        (pltpu.VMEM((rows, cols), BF16), pltpu.VMEM((1, rows, width), BF16)),
        [vmem_spec()] * 4,
        [],
        2 * rows * cols * width,
        2 * cols * width,
        "mix",
    )(weights, out, mem_val, w_out)


def rest_kernel(others, kept, head_ref, w_ref, away_ref, keep_ref):
    blocks_out(True, others, head_ref[...], w_ref, away_ref)
    blocks_out(False, kept, head_ref[...], w_ref, keep_ref)


def rest(others, kept, head_out, w_out, width):
    rows, cols = head_out.shape
    return call(
        functools.partial(rest_kernel, others, kept),
        (
            pltpu.VMEM((len(others), rows, width), BF16),
            pltpu.VMEM((len(kept), rows, width), F32),
        ),
        [vmem_spec()] * 2,
        [],
        4 * rows * cols * width * len(kept),
        4 * cols * width * len(kept),
        "rest",
    )(head_out, w_out)


def total_kernel(own_ref, *refs):
    out_ref, buf, sem = refs[-3:]
    total = own_ref[...]
    for term in refs[:-3]:
        total = total + term[...].astype(F32)
    buf[...] = total.astype(BF16)
    copy = pltpu.make_async_copy(buf, out_ref, sem)
    copy.start()
    copy.wait()


def total_sum(own, terms):
    return pl.pallas_call(
        total_kernel,
        out_shape=jax.ShapeDtypeStruct(own.shape, BF16),
        in_specs=[vmem_spec()] * (1 + len(terms)),
        out_specs=hbm_spec(),
        scratch_shapes=[pltpu.VMEM(own.shape, BF16), pltpu.SemaphoreType.DMA],
        compiler_params=pltpu.CompilerParams(vmem_limit_bytes=VMEM_LIMIT),
        name="total",
    )(own, *terms)


def shards(tokens, w_qkv, w_pos, w_out, content_bias, position_bias, doc_ids):
    rows = tokens.shape[0]
    count = lax.axis_size("mp")
    chips = count // 2
    segments = lax.axis_size("seq")
    width = w_out.shape[1] // count

    def across(value, k):
        return lax.ppermute(value, "mp", [(i, (i + 2 * k) % count) for i in range(count)])

    def swap(value):
        return lax.ppermute(value, "mp", [(i, i ^ 1) for i in range(count)])

    def onward(value):
        return lax.ppermute(value, "seq", [(i, (i + 1) % segments) for i in range(segments)])

    mine = [tokens] + [across(tokens, k) for k in range(1, chips)]
    other = [swap(tokens)]
    docs = (doc_ids + 1).astype(F32).reshape(1, rows)
    rel, w_kv = load(w_pos, w_qkv, 2 * rows)
    for k in range(1, chips):
        mine[k], rel = lax.optimization_barrier((mine[k], rel))
        other.append(swap(mine[k]))
    last = chips - 1
    acc = None
    for k in range(last):
        part = {(k, 0): mine[k], (k, 1): other[k]}
        if k == last - 1:
            part[last, 0] = mine[last]
        acc = kv_step(part, w_kv, acc)
    part = {(last, 1): other[last]}
    own_key = kv_step(part, w_kv, acc, (1,), "keys", docs, content_bias.shape[0])
    mem_key = onward(own_key)
    own_val = kv_step(part, w_kv, acc, (2,), "values")
    mem_val = onward(own_val)
    own_val, rel = lax.optimization_barrier((own_val, rel))
    query_content, score, w_out = queries(
        [chunk for pair in zip(mine, other) for chunk in pair],
        w_qkv,
        w_out,
        content_bias,
        position_bias,
        own_key,
        rel,
        docs,
    )
    weights, out = weigh(query_content, score, mem_key, own_val, docs)
    first = chips // 2
    others = [k for k in range(chips) if k != first]
    head_out, away = mix(first, weights, out, mem_val, w_out, width)
    swapped = swap(away)
    away, keep = rest(others, [first] + others, head_out, w_out, width)
    total = {first: keep[0] + swapped[0].astype(F32)}
    away, total[first] = lax.optimization_barrier((away, total[first]))
    away = swap(away)
    for i, k in enumerate(others):
        total[k] = keep[i + 1] + away[i].astype(F32)
    terms = [across(total[k].astype(BF16), k) for k in [first] + others if k > 0]
    return total_sum(total[0], terms)


def solution(mesh):
    in_specs = (
        P("seq", "mp"),
        P(None, None, "mp"),
        P(None, "mp"),
        P("mp", None),
        P("mp", None),
        P("mp", None),
        P("seq"),
    )
    out_specs = P("seq", "mp")
    return jax.shard_map(shards, mesh=mesh, in_specs=in_specs, out_specs=out_specs, check_vma=False)
```

```python
import functools

import jax
import jax.numpy as jnp
from jax import lax
from jax.experimental import pallas as pl
from jax.experimental.pallas import tpu as pltpu
from jax.sharding import PartitionSpec as P

BF16 = jnp.bfloat16
F32 = jnp.float32
VMEM_LIMIT = 16 * 1024 * 1024


def vmem_spec():
    return pl.BlockSpec(memory_space=pltpu.VMEM)


def hbm_spec():
    return pl.BlockSpec(memory_space=pl.ANY)


def in_hbm(value):
    return pltpu.with_memory_space_constraint(value, pltpu.HBM)


def call(kernel, out_shape, in_specs, scratch, flops, nbytes, name, transcendentals=0):
    outs = jax.tree.map(lambda _: vmem_spec(), out_shape)
    return pl.pallas_call(
        kernel,
        out_shape=out_shape,
        in_specs=in_specs,
        out_specs=outs,
        scratch_shapes=scratch,
        compiler_params=pltpu.CompilerParams(vmem_limit_bytes=VMEM_LIMIT),
        cost_estimate=pl.CostEstimate(
            flops=flops, bytes_accessed=nbytes, transcendentals=transcendentals
        ),
        name=name,
    )


def dot(a, b):
    return jnp.dot(a, b, preferred_element_type=F32)


def dot_nt(a, b):
    return lax.dot_general(a, b, (((1,), (1,)), ((), ())), preferred_element_type=F32)


def load_kernel(parts, w_pos, w_qkv, rel_ref, kv_ref, wbuf, table, sems):
    rows, cols = rel_ref.shape
    width = w_pos.shape[0]
    half = width // 2
    depth = width // parts

    def pos_copy(i):
        part = pl.ds(i * depth, depth)
        return pltpu.make_async_copy(w_pos.at[part], wbuf.at[part], sems.at[i])

    copies = [pos_copy(i) for i in range(parts)]
    for c in range(2):
        copies.append(pltpu.make_async_copy(w_qkv.at[c + 1], kv_ref.at[c], sems.at[parts + c]))
    for item in copies:
        item.start()
    fine = 16
    coarse = rows // fine
    index = lax.broadcasted_iota(jnp.int32, (1, half), 1).astype(F32) * 2.0
    freqs = 1.0 / 10000.0 ** (index / width)
    low = (fine - 1 - lax.broadcasted_iota(jnp.int32, (fine, half), 0)).astype(F32) * freqs
    high = (lax.broadcasted_iota(jnp.int32, (coarse, half), 0) * fine).astype(F32) * freqs
    sin_low, cos_low = jnp.sin(low), jnp.cos(low)
    sin_high, cos_high = jnp.sin(high), jnp.cos(high)
    for a in range(coarse):
        sh, ch = sin_high[a : a + 1], cos_high[a : a + 1]
        first = (coarse - 1 - a) * fine
        table[first : first + fine, :half] = (sh * cos_low + ch * sin_low).astype(BF16)
        table[first : first + fine, half:] = (ch * cos_low - sh * sin_low).astype(BF16)
    total = jnp.zeros((rows, cols), F32)
    for i in range(parts):
        copies[i].wait()
        total = total + dot(
            table[:, i * depth : (i + 1) * depth], wbuf[i * depth : (i + 1) * depth]
        )
    rel_ref[...] = total.astype(BF16)
    for item in copies[parts:]:
        item.wait()


def load(w_pos, w_qkv, rows):
    width, cols = w_pos.shape
    parts = 8
    return call(
        functools.partial(load_kernel, parts),
        (pltpu.VMEM((rows, cols), BF16), pltpu.VMEM((2, width, cols), BF16)),
        [hbm_spec()] * 2,
        [
            pltpu.VMEM((width, cols), BF16),
            pltpu.VMEM((rows, width), BF16),
            pltpu.SemaphoreType.DMA((parts + 2,)),
        ],
        rows * width,
        rows * width,
        "load",
    )(in_hbm(w_pos), in_hbm(w_qkv))


def here(back):
    me = lax.axis_index("mp")
    chips = lax.axis_size("mp") // 2
    return lax.rem(me, 2), lax.rem(me // 2 + chips - back, chips)


def row_block(core, place, i):
    return 2 * place + (core if i == 0 else 1 - core)


def kv_kernel(sources, kinds, first, last, *refs):
    refs = list(refs)
    x_refs = [refs.pop(0) for _ in sources]
    w_ref = refs.pop(0)
    acc_ref = None if first else refs.pop(0)
    doc_ref = refs.pop(0) if last == "keys" else None
    (out_ref,) = refs
    rows, depth = x_refs[0].shape
    for kind in kinds:
        total = None if first else acc_ref[kind - 1]
        for (back, i), x_ref in zip(sources, x_refs):
            core, place = here(back)
            start = pl.multiple_of(row_block(core, place, i) * depth, depth)
            term = dot(x_ref[...], w_ref[kind - 1, pl.ds(start, depth)])
            total = term if total is None else total + term
        if last == "keys":
            head_dim = out_ref.shape[1]
            for h in range(total.shape[1] // head_dim):
                part = total[:, h * head_dim : (h + 1) * head_dim]
                out_ref[h * rows : (h + 1) * rows] = part.astype(BF16)
            docs = jnp.broadcast_to(doc_ref[...], (16, rows)).astype(BF16)
            out_ref[out_ref.shape[0] - 16 :] = docs
        elif last == "values":
            out_ref[...] = total.astype(BF16)
        else:
            out_ref[kind - 1] = total


def kv_step(chunks, w_qkv, acc, kinds=(1, 2), last=None, docs=None, heads=None):
    sources = tuple(chunks)
    rows, depth = chunks[sources[0]].shape
    cols = w_qkv.shape[2]
    args = [chunks[source] for source in sources] + [w_qkv]
    args += ([] if acc is None else [acc]) + ([] if docs is None else [docs])
    out = pltpu.VMEM((2, rows, cols), F32)
    if last == "keys":
        assert rows == cols // heads
        out = pltpu.VMEM((heads * rows + 16, cols // heads), BF16)
    elif last == "values":
        out = pltpu.VMEM((rows, cols), BF16)
    return call(
        functools.partial(kv_kernel, sources, kinds, acc is None, last),
        out,
        [vmem_spec()] * len(args),
        [],
        16 * rows * depth * cols,
        0,
        "kv_step",
    )(*args)


def q_kernel(count, heads, *refs):
    x_refs = refs[:count]
    w_ref, w_out, cb_ref, pb_ref, key_ref, rel_ref, doc_ref = refs[count : count + 7]
    qc_ref, score_ref, w_out_ref, wbuf, sems = refs[count + 7 :]
    rows, depth = x_refs[0].shape
    head_dim = qc_ref.shape[1] // heads

    def copy(i):
        core, place = here(i // 2)
        start = pl.multiple_of(row_block(core, place, i % 2) * depth, depth)
        return pltpu.make_async_copy(w_ref.at[0, pl.ds(start, depth)], wbuf.at[i], sems.at[i])

    copies = [copy(i) for i in range(count)]
    copies.append(pltpu.make_async_copy(w_out, w_out_ref, sems.at[count]))
    for item in copies:
        item.start()
    total = None
    for i in range(count):
        copies[i].wait()
        term = dot(x_refs[i][...], wbuf[i])
        total = term if total is None else total + term
    query_content = (total + cb_ref[...]).astype(BF16)
    query_pos = (total + pb_ref[...]).astype(BF16)
    qc_ref[...] = query_content
    query = lax.broadcasted_iota(jnp.int32, (rows, rows), 0)
    key = lax.broadcasted_iota(jnp.int32, (rows, rows), 1)
    own_doc = jnp.broadcast_to(doc_ref[...], (rows, rows))
    allowed = (key <= query) & (own_doc == own_doc.T)
    scale = 1.0 / (float(head_dim) ** 0.5)
    for h in range(heads):
        part = slice(h * head_dim, (h + 1) * head_dim)
        pos = pltpu.roll(
            dot_nt(query_pos[:, part], rel_ref[:, part]), rows + 1, 1, stride=1, stride_axis=0
        )
        content = dot_nt(query_content[:, part], key_ref[h * rows : (h + 1) * rows])
        score_ref[h, :, :rows] = pos[:, :rows]
        score_ref[h, :, rows:] = jnp.where(allowed, (content + pos[:, rows:]) * scale, -1e30)
    copies[count].wait()


def queries(chunks, w_qkv, w_out, content_bias, position_bias, own_key, rel, docs):
    count = len(chunks)
    rows, depth = chunks[0].shape
    cols = w_qkv.shape[2]
    heads = content_bias.shape[0]
    return call(
        functools.partial(q_kernel, count, heads),
        (
            pltpu.VMEM((rows, cols), BF16),
            pltpu.VMEM((heads, rows, 2 * rows), F32),
            pltpu.VMEM(w_out.shape, BF16),
        ),
        [vmem_spec()] * count + [hbm_spec()] * 2 + [vmem_spec()] * 5,
        [pltpu.VMEM((count, depth, cols), BF16), pltpu.SemaphoreType.DMA((count + 1,))],
        2 * count * rows * depth * cols,
        2 * count * depth * cols,
        "queries",
    )(
        *chunks,
        in_hbm(w_qkv),
        in_hbm(w_out),
        content_bias.reshape(1, cols),
        position_bias.reshape(1, cols),
        own_key,
        rel,
        docs,
    )


def weigh_kernel(qc_ref, score_ref, mem_ref, val_ref, doc_ref, weight_ref, out_ref):
    heads, rows, _ = score_ref.shape
    head_dim = qc_ref.shape[1] // heads
    exists = jnp.minimum(lax.axis_index("seq"), 1).astype(F32)
    mem_doc = mem_ref[heads * rows : heads * rows + 16].astype(F32)[:1] * exists
    mem_doc = jnp.broadcast_to(mem_doc, (rows, rows))
    allowed = mem_doc == jnp.broadcast_to(doc_ref[...], (rows, rows)).T
    scale = 1.0 / (float(head_dim) ** 0.5)
    for h in range(heads):
        part = slice(h * head_dim, (h + 1) * head_dim)
        content = dot_nt(qc_ref[:, part], mem_ref[h * rows : (h + 1) * rows])
        mem = jnp.where(allowed, (content + score_ref[h, :, :rows]) * scale, -1e30)
        own = score_ref[h, :, rows:]
        top = jnp.maximum(
            jnp.max(mem, axis=1, keepdims=True), jnp.max(own, axis=1, keepdims=True)
        )
        mem = jnp.where(mem > -1e29, jnp.exp(mem - top), 0.0)
        own = jnp.where(own > -1e29, jnp.exp(own - top), 0.0)
        total = jnp.sum(mem, axis=1, keepdims=True) + jnp.sum(own, axis=1, keepdims=True)
        weight_ref[h] = (mem / total).astype(BF16)
        out_ref[:, part] = dot((own / total).astype(BF16), val_ref[:, part])


def weigh(query_content, score, mem_key, own_val, docs):
    rows, cols = query_content.shape
    heads = score.shape[0]
    return call(
        weigh_kernel,
        (pltpu.VMEM((heads, rows, rows), BF16), pltpu.VMEM((rows, cols), F32)),
        [vmem_spec()] * 5,
        [],
        8 * rows * rows * cols,
        8 * rows * cols,
        "weigh",
    )(query_content, score, mem_key, own_val, docs)


def blocks_out(away, offsets, head_out, w_ref, out_ref):
    width = out_ref.shape[2]
    core, chip = here(0)
    chips = lax.axis_size("mp") // 2
    for i, k in enumerate(offsets):
        block = 2 * lax.rem(chip + k, chips) + (1 - core if away else core)
        start = pl.multiple_of(block * width, width)
        out_ref[i] = dot(head_out, w_ref[:, pl.ds(start, width)]).astype(out_ref.dtype)


def mix_kernel(first, weight_ref, out_ref, mem_ref, w_ref, head_ref, away_ref):
    heads, rows, _ = weight_ref.shape
    head_dim = out_ref.shape[1] // heads
    for h in range(heads):
        part = slice(h * head_dim, (h + 1) * head_dim)
        out = out_ref[:, part] + dot(weight_ref[h], mem_ref[:, part])
        head_ref[:, part] = out.astype(BF16)
    blocks_out(True, [first], head_ref[...], w_ref, away_ref)


def mix(first, weights, out, mem_val, w_out, width):
    rows, cols = out.shape
    return call(
        functools.partial(mix_kernel, first),
        (pltpu.VMEM((rows, cols), BF16), pltpu.VMEM((1, rows, width), BF16)),
        [vmem_spec()] * 4,
        [],
        2 * rows * cols * width,
        2 * cols * width,
        "mix",
    )(weights, out, mem_val, w_out)


def rest_kernel(others, kept, head_ref, w_ref, away_ref, keep_ref):
    blocks_out(True, others, head_ref[...], w_ref, away_ref)
    blocks_out(False, kept, head_ref[...], w_ref, keep_ref)


def rest(others, kept, head_out, w_out, width):
    rows, cols = head_out.shape
    return call(
        functools.partial(rest_kernel, others, kept),
        (
            pltpu.VMEM((len(others), rows, width), BF16),
            pltpu.VMEM((len(kept), rows, width), F32),
        ),
        [vmem_spec()] * 2,
        [],
        4 * rows * cols * width * len(kept),
        4 * cols * width * len(kept),
        "rest",
    )(head_out, w_out)


def shards(tokens, w_qkv, w_pos, w_out, content_bias, position_bias, doc_ids):
    rows = tokens.shape[0]
    count = lax.axis_size("mp")
    chips = count // 2
    segments = lax.axis_size("seq")
    width = w_out.shape[1] // count

    def across(value, k):
        return lax.ppermute(value, "mp", [(i, (i + 2 * k) % count) for i in range(count)])

    def swap(value):
        return lax.ppermute(value, "mp", [(i, i ^ 1) for i in range(count)])

    def onward(value):
        return lax.ppermute(value, "seq", [(i, (i + 1) % segments) for i in range(segments)])

    mine = [tokens] + [across(tokens, k) for k in range(1, chips)]
    other = [swap(tokens)]
    docs = (doc_ids + 1).astype(F32).reshape(1, rows)
    rel, w_kv = load(w_pos, w_qkv, 2 * rows)
    for k in range(1, chips):
        mine[k], rel = lax.optimization_barrier((mine[k], rel))
        other.append(swap(mine[k]))
    last = chips - 1
    acc = None
    for k in range(last):
        acc = kv_step({(k, 0): mine[k], (k, 1): other[k]}, w_kv, acc)
    part = {(last, 0): mine[last], (last, 1): other[last]}
    own_key = kv_step(part, w_kv, acc, (1,), "keys", docs, content_bias.shape[0])
    mem_key = onward(own_key)
    own_val = kv_step(part, w_kv, acc, (2,), "values")
    mem_val = onward(own_val)
    own_val, rel = lax.optimization_barrier((own_val, rel))
    query_content, score, w_out = queries(
        [chunk for pair in zip(mine, other) for chunk in pair],
        w_qkv,
        w_out,
        content_bias,
        position_bias,
        own_key,
        rel,
        docs,
    )
    weights, out = weigh(query_content, score, mem_key, own_val, docs)
    first = chips // 2
    others = [k for k in range(chips) if k != first]
    head_out, away = mix(first, weights, out, mem_val, w_out, width)
    swapped = swap(away)
    away, keep = rest(others, [first] + others, head_out, w_out, width)
    total = {first: keep[0] + swapped[0].astype(F32)}
    away, total[first] = lax.optimization_barrier((away, total[first]))
    away = swap(away)
    for i, k in enumerate(others):
        total[k] = keep[i + 1] + away[i].astype(F32)
    result = total[0]
    for k in [first] + others:
        if k > 0:
            result = result + across(total[k].astype(BF16), k).astype(F32)
    return result.astype(BF16)


def solution(mesh):
    in_specs = (
        P("seq", "mp"),
        P(None, None, "mp"),
        P(None, "mp"),
        P("mp", None),
        P("mp", None),
        P("mp", None),
        P("seq"),
    )
    out_specs = P("seq", "mp")
    return jax.shard_map(shards, mesh=mesh, in_specs=in_specs, out_specs=out_specs, check_vma=False)
```

```python
import functools

import jax
import jax.numpy as jnp
from jax import lax
from jax.experimental import pallas as pl
from jax.experimental.pallas import tpu as pltpu
from jax.sharding import PartitionSpec as P

BF16 = jnp.bfloat16
F32 = jnp.float32
VMEM_LIMIT = 16 * 1024 * 1024


def vmem_spec():
    return pl.BlockSpec(memory_space=pltpu.VMEM)


def hbm_spec():
    return pl.BlockSpec(memory_space=pl.ANY)


def in_hbm(value):
    return pltpu.with_memory_space_constraint(value, pltpu.HBM)


def call(kernel, out_shape, in_specs, scratch, flops, nbytes, name, transcendentals=0):
    outs = jax.tree.map(lambda _: vmem_spec(), out_shape)
    return pl.pallas_call(
        kernel,
        out_shape=out_shape,
        in_specs=in_specs,
        out_specs=outs,
        scratch_shapes=scratch,
        compiler_params=pltpu.CompilerParams(vmem_limit_bytes=VMEM_LIMIT),
        cost_estimate=pl.CostEstimate(
            flops=flops, bytes_accessed=nbytes, transcendentals=transcendentals
        ),
        name=name,
    )


def dot(a, b):
    return jnp.dot(a, b, preferred_element_type=F32)


def dot_nt(a, b):
    return lax.dot_general(a, b, (((1,), (1,)), ((), ())), preferred_element_type=F32)


def load_kernel(parts, w_pos, w_qkv, rel_ref, kv_ref, wbuf, table, sems):
    rows, cols = rel_ref.shape
    width = w_pos.shape[0]
    half = width // 2
    depth = width // parts

    def pos_copy(i):
        part = pl.ds(i * depth, depth)
        return pltpu.make_async_copy(w_pos.at[part], wbuf.at[part], sems.at[i])

    copies = [pos_copy(i) for i in range(parts)]
    for c in range(2):
        copies.append(pltpu.make_async_copy(w_qkv.at[c + 1], kv_ref.at[c], sems.at[parts + c]))
    for item in copies:
        item.start()
    fine = 16
    coarse = rows // fine
    index = lax.broadcasted_iota(jnp.int32, (1, half), 1).astype(F32) * 2.0
    freqs = 1.0 / 10000.0 ** (index / width)
    low = (fine - 1 - lax.broadcasted_iota(jnp.int32, (fine, half), 0)).astype(F32) * freqs
    high = (lax.broadcasted_iota(jnp.int32, (coarse, half), 0) * fine).astype(F32) * freqs
    sin_low, cos_low = jnp.sin(low), jnp.cos(low)
    sin_high, cos_high = jnp.sin(high), jnp.cos(high)
    for a in range(coarse):
        sh, ch = sin_high[a : a + 1], cos_high[a : a + 1]
        first = (coarse - 1 - a) * fine
        table[first : first + fine, :half] = (sh * cos_low + ch * sin_low).astype(BF16)
        table[first : first + fine, half:] = (ch * cos_low - sh * sin_low).astype(BF16)
    total = jnp.zeros((rows, cols), F32)
    for i in range(parts):
        copies[i].wait()
        total = total + dot(
            table[:, i * depth : (i + 1) * depth], wbuf[i * depth : (i + 1) * depth]
        )
    rel_ref[...] = total.astype(BF16)
    for item in copies[parts:]:
        item.wait()


def load(w_pos, w_qkv, rows):
    width, cols = w_pos.shape
    parts = 8
    return call(
        functools.partial(load_kernel, parts),
        (pltpu.VMEM((rows, cols), BF16), pltpu.VMEM((2, width, cols), BF16)),
        [hbm_spec()] * 2,
        [
            pltpu.VMEM((width, cols), BF16),
            pltpu.VMEM((rows, width), BF16),
            pltpu.SemaphoreType.DMA((parts + 2,)),
        ],
        rows * width,
        rows * width,
        "load",
    )(in_hbm(w_pos), in_hbm(w_qkv))


def here(back):
    me = lax.axis_index("mp")
    chips = lax.axis_size("mp") // 2
    return lax.rem(me, 2), lax.rem(me // 2 + chips - back, chips)


def row_block(core, place, i):
    return 2 * place + (core if i == 0 else 1 - core)


def kv_kernel(sources, kinds, first, last, *refs):
    refs = list(refs)
    x_refs = [refs.pop(0) for _ in sources]
    w_ref = refs.pop(0)
    acc_ref = None if first else refs.pop(0)
    doc_ref = refs.pop(0) if last == "keys" else None
    out_ref = refs[0]
    rows, depth = x_refs[0].shape
    for kind in kinds:
        total = None if first else acc_ref[kind - 1]
        for (back, i), x_ref in zip(sources, x_refs):
            core, place = here(back)
            start = pl.multiple_of(row_block(core, place, i) * depth, depth)
            term = dot(x_ref[...], w_ref[kind - 1, pl.ds(start, depth)])
            total = term if total is None else total + term
        if last == "keys" and kind == 2:
            refs[1][...] = total.astype(BF16)
        elif last == "keys":
            head_dim = out_ref.shape[1]
            for h in range(total.shape[1] // head_dim):
                part = total[:, h * head_dim : (h + 1) * head_dim]
                out_ref[h * rows : (h + 1) * rows] = part.astype(BF16)
            docs = jnp.broadcast_to(doc_ref[...], (16, rows)).astype(BF16)
            out_ref[out_ref.shape[0] - 16 :] = docs
        else:
            out_ref[kind - 1] = total


def kv_step(chunks, w_qkv, acc, kinds=(1, 2), last=None, docs=None, heads=None):
    sources = tuple(chunks)
    rows, depth = chunks[sources[0]].shape
    cols = w_qkv.shape[2]
    args = [chunks[source] for source in sources] + [w_qkv]
    args += ([] if acc is None else [acc]) + ([] if docs is None else [docs])
    out = pltpu.VMEM((2, rows, cols), F32)
    if last == "keys":
        assert rows == cols // heads
        out = (
            pltpu.VMEM((heads * rows + 16, cols // heads), BF16),
            pltpu.VMEM((rows, cols), BF16),
        )
    return call(
        functools.partial(kv_kernel, sources, kinds, acc is None, last),
        out,
        [vmem_spec()] * len(args),
        [],
        16 * rows * depth * cols,
        0,
        "kv_step",
    )(*args)


def q_kernel(count, heads, *refs):
    x_refs = refs[:count]
    w_ref, w_out, cb_ref, pb_ref, key_ref, rel_ref, doc_ref = refs[count : count + 7]
    qc_ref, score_ref, w_out_ref, wbuf, sems = refs[count + 7 :]
    rows, depth = x_refs[0].shape
    head_dim = qc_ref.shape[1] // heads

    def copy(i):
        core, place = here(i // 2)
        start = pl.multiple_of(row_block(core, place, i % 2) * depth, depth)
        return pltpu.make_async_copy(w_ref.at[0, pl.ds(start, depth)], wbuf.at[i], sems.at[i])

    copies = [copy(i) for i in range(count)]
    copies.append(pltpu.make_async_copy(w_out, w_out_ref, sems.at[count]))
    for item in copies:
        item.start()
    total = None
    for i in range(count):
        copies[i].wait()
        term = dot(x_refs[i][...], wbuf[i])
        total = term if total is None else total + term
    query_content = (total + cb_ref[...]).astype(BF16)
    query_pos = (total + pb_ref[...]).astype(BF16)
    qc_ref[...] = query_content
    query = lax.broadcasted_iota(jnp.int32, (rows, rows), 0)
    key = lax.broadcasted_iota(jnp.int32, (rows, rows), 1)
    own_doc = jnp.broadcast_to(doc_ref[...], (rows, rows))
    allowed = (key <= query) & (own_doc == own_doc.T)
    scale = 1.0 / (float(head_dim) ** 0.5)
    for h in range(heads):
        part = slice(h * head_dim, (h + 1) * head_dim)
        pos = pltpu.roll(
            dot_nt(query_pos[:, part], rel_ref[:, part]), rows + 1, 1, stride=1, stride_axis=0
        )
        content = dot_nt(query_content[:, part], key_ref[h * rows : (h + 1) * rows])
        score_ref[h, :, :rows] = pos[:, :rows]
        score_ref[h, :, rows:] = jnp.where(allowed, (content + pos[:, rows:]) * scale, -1e30)
    copies[count].wait()


def queries(chunks, w_qkv, w_out, content_bias, position_bias, own_key, rel, docs):
    count = len(chunks)
    rows, depth = chunks[0].shape
    cols = w_qkv.shape[2]
    heads = content_bias.shape[0]
    return call(
        functools.partial(q_kernel, count, heads),
        (
            pltpu.VMEM((rows, cols), BF16),
            pltpu.VMEM((heads, rows, 2 * rows), F32),
            pltpu.VMEM(w_out.shape, BF16),
        ),
        [vmem_spec()] * count + [hbm_spec()] * 2 + [vmem_spec()] * 5,
        [pltpu.VMEM((count, depth, cols), BF16), pltpu.SemaphoreType.DMA((count + 1,))],
        2 * count * rows * depth * cols,
        2 * count * depth * cols,
        "queries",
    )(
        *chunks,
        in_hbm(w_qkv),
        in_hbm(w_out),
        content_bias.reshape(1, cols),
        position_bias.reshape(1, cols),
        own_key,
        rel,
        docs,
    )


def weigh_kernel(qc_ref, score_ref, mem_ref, val_ref, doc_ref, weight_ref, out_ref):
    heads, rows, _ = score_ref.shape
    head_dim = qc_ref.shape[1] // heads
    exists = jnp.minimum(lax.axis_index("seq"), 1).astype(F32)
    mem_doc = mem_ref[heads * rows : heads * rows + 16].astype(F32)[:1] * exists
    mem_doc = jnp.broadcast_to(mem_doc, (rows, rows))
    allowed = mem_doc == jnp.broadcast_to(doc_ref[...], (rows, rows)).T
    scale = 1.0 / (float(head_dim) ** 0.5)
    for h in range(heads):
        part = slice(h * head_dim, (h + 1) * head_dim)
        content = dot_nt(qc_ref[:, part], mem_ref[h * rows : (h + 1) * rows])
        mem = jnp.where(allowed, (content + score_ref[h, :, :rows]) * scale, -1e30)
        own = score_ref[h, :, rows:]
        top = jnp.maximum(
            jnp.max(mem, axis=1, keepdims=True), jnp.max(own, axis=1, keepdims=True)
        )
        mem = jnp.where(mem > -1e29, jnp.exp(mem - top), 0.0)
        own = jnp.where(own > -1e29, jnp.exp(own - top), 0.0)
        total = jnp.sum(mem, axis=1, keepdims=True) + jnp.sum(own, axis=1, keepdims=True)
        weight_ref[h] = (mem / total).astype(BF16)
        out_ref[:, part] = dot((own / total).astype(BF16), val_ref[:, part])


def weigh(query_content, score, mem_key, own_val, docs):
    rows, cols = query_content.shape
    heads = score.shape[0]
    return call(
        weigh_kernel,
        (pltpu.VMEM((heads, rows, rows), BF16), pltpu.VMEM((rows, cols), F32)),
        [vmem_spec()] * 5,
        [],
        8 * rows * rows * cols,
        8 * rows * cols,
        "weigh",
    )(query_content, score, mem_key, own_val, docs)


def blocks_out(away, offsets, head_out, w_ref, out_ref):
    width = out_ref.shape[2]
    core, chip = here(0)
    chips = lax.axis_size("mp") // 2
    for i, k in enumerate(offsets):
        block = 2 * lax.rem(chip + k, chips) + (1 - core if away else core)
        start = pl.multiple_of(block * width, width)
        out_ref[i] = dot(head_out, w_ref[:, pl.ds(start, width)]).astype(out_ref.dtype)


def mix_kernel(first, weight_ref, out_ref, mem_ref, w_ref, head_ref, away_ref):
    heads, rows, _ = weight_ref.shape
    head_dim = out_ref.shape[1] // heads
    for h in range(heads):
        part = slice(h * head_dim, (h + 1) * head_dim)
        out = out_ref[:, part] + dot(weight_ref[h], mem_ref[:, part])
        head_ref[:, part] = out.astype(BF16)
    blocks_out(True, [first], head_ref[...], w_ref, away_ref)


def mix(first, weights, out, mem_val, w_out, width):
    rows, cols = out.shape
    return call(
        functools.partial(mix_kernel, first),
        (pltpu.VMEM((rows, cols), BF16), pltpu.VMEM((1, rows, width), BF16)),
        [vmem_spec()] * 4,
        [],
        2 * rows * cols * width,
        2 * cols * width,
        "mix",
    )(weights, out, mem_val, w_out)


def rest_kernel(others, kept, head_ref, w_ref, away_ref, keep_ref):
    blocks_out(True, others, head_ref[...], w_ref, away_ref)
    blocks_out(False, kept, head_ref[...], w_ref, keep_ref)


def rest(others, kept, head_out, w_out, width):
    rows, cols = head_out.shape
    return call(
        functools.partial(rest_kernel, others, kept),
        (
            pltpu.VMEM((len(others), rows, width), BF16),
            pltpu.VMEM((len(kept), rows, width), F32),
        ),
        [vmem_spec()] * 2,
        [],
        4 * rows * cols * width * len(kept),
        4 * cols * width * len(kept),
        "rest",
    )(head_out, w_out)


def total_kernel(own_ref, *refs):
    out_ref, buf, sem = refs[-3:]
    total = own_ref[...]
    for term in refs[:-3]:
        total = total + term[...].astype(F32)
    buf[...] = total.astype(BF16)
    copy = pltpu.make_async_copy(buf, out_ref, sem)
    copy.start()
    copy.wait()


def total_sum(own, terms):
    return pl.pallas_call(
        total_kernel,
        out_shape=jax.ShapeDtypeStruct(own.shape, BF16),
        in_specs=[vmem_spec()] * (1 + len(terms)),
        out_specs=hbm_spec(),
        scratch_shapes=[pltpu.VMEM(own.shape, BF16), pltpu.SemaphoreType.DMA],
        compiler_params=pltpu.CompilerParams(vmem_limit_bytes=VMEM_LIMIT),
        name="total",
    )(own, *terms)


def shards(tokens, w_qkv, w_pos, w_out, content_bias, position_bias, doc_ids):
    rows = tokens.shape[0]
    count = lax.axis_size("mp")
    chips = count // 2
    segments = lax.axis_size("seq")
    width = w_out.shape[1] // count

    def across(value, k):
        return lax.ppermute(value, "mp", [(i, (i + 2 * k) % count) for i in range(count)])

    def swap(value):
        return lax.ppermute(value, "mp", [(i, i ^ 1) for i in range(count)])

    def onward(value):
        return lax.ppermute(value, "seq", [(i, (i + 1) % segments) for i in range(segments)])

    mine = [tokens] + [across(tokens, k) for k in range(1, chips)]
    other = [swap(tokens)]
    docs = (doc_ids + 1).astype(F32).reshape(1, rows)
    rel, w_kv = load(w_pos, w_qkv, 2 * rows)
    for k in range(1, chips):
        mine[k], rel = lax.optimization_barrier((mine[k], rel))
        other.append(swap(mine[k]))
    last = chips - 1
    acc = None
    for k in range(last):
        part = {(k, 0): mine[k], (k, 1): other[k]}
        if k == last - 1:
            part[last, 0] = mine[last]
        acc = kv_step(part, w_kv, acc)
    part = {(last, 1): other[last]}
    own_key, own_val = kv_step(
        part, w_kv, acc, (1, 2), "keys", docs, content_bias.shape[0]
    )
    mem_key = onward(own_key)
    mem_val = onward(own_val)
    own_val, rel = lax.optimization_barrier((own_val, rel))
    query_content, score, w_out = queries(
        [chunk for pair in zip(mine, other) for chunk in pair],
        w_qkv,
        w_out,
        content_bias,
        position_bias,
        own_key,
        rel,
        docs,
    )
    weights, out = weigh(query_content, score, mem_key, own_val, docs)
    first = chips // 2
    others = [k for k in range(chips) if k != first]
    head_out, away = mix(first, weights, out, mem_val, w_out, width)
    swapped = swap(away)
    away, keep = rest(others, [first] + others, head_out, w_out, width)
    total = {first: keep[0] + swapped[0].astype(F32)}
    away, total[first] = lax.optimization_barrier((away, total[first]))
    away = swap(away)
    for i, k in enumerate(others):
        total[k] = keep[i + 1] + away[i].astype(F32)
    terms = [across(total[k].astype(BF16), k) for k in [first] + others if k > 0]
    return total_sum(total[0], terms)


def solution(mesh):
    in_specs = (
        P("seq", "mp"),
        P(None, None, "mp"),
        P(None, "mp"),
        P("mp", None),
        P("mp", None),
        P("mp", None),
        P("seq"),
    )
    out_specs = P("seq", "mp")
    return jax.shard_map(shards, mesh=mesh, in_specs=in_specs, out_specs=out_specs, check_vma=False)
```
